32 devices in a mesh: groups: 2 (over y), gx: 16 (over z, x, core).
Axes of the slice: x: 2, y: 2, z: 4, core: 2. Of those that a mesh axis runs over, the one named last changes fastest.
Arguments:
- tokens: bfloat16 [2, 32, 18432], P(None, ('groups', 'gx')), parts along dimension 1, may hold values from -6 to 6
- norm_gain: float32 [18432], replicated, may hold values from 0.1 to 1.9
- w_query: bfloat16 [6144, 18432], P('gx'), may hold values from -0.046875 to 0.046875
- w_keyval: bfloat16 [512, 18432], P('gx'), may hold values from -0.046875 to 0.046875
- w_gate: bfloat16 [9216, 18432], P('gx'), may hold values from -0.046875 to 0.046875
- w_up: bfloat16 [9216, 18432], P('gx'), may hold values from -0.046875 to 0.046875
- w_out: bfloat16 [6144, 18432], P('gx'), may hold values from -0.078125 to 0.078125
- w_down: bfloat16 [9216, 18432], P('gx'), may hold values from -0.0625 to 0.0625
- cache_keys: bfloat16 [32, 1024, 256], P(('groups', 'gx')), parts along dimension 0
- cache_values: bfloat16 [32, 1024, 256], P(('groups', 'gx')), parts along dimension 0, may hold values from -6 to 6
- lengths: int32 [32], P(('groups', 'gx')), parts along dimension 0, may hold values from 128 to 1024, as said below
- positions: int32 [32], P(('groups', 'gx')), parts along dimension 0, may hold values from 1024 to 4095
Outputs:
- layer_out: bfloat16 [2, 32, 18432], P(None, ('groups', 'gx')), parts along dimension 1
The draws below stay inside these ranges and needn't reach their ends.
There are 2 independent parts, one for each index of `groups`. The reference program is written for one: setup_inputs(seed, part) draws one part's arguments, and reference() takes and returns one part's arrays. A program takes and returns all parts, laid end to end along the dimension named above; an argument that names none is the same for every part. Nothing has to cross between parts.
Inputs may be any that keep to these rules, and one draw needn't show every extreme that they name: `lengths`: some row has all 1024 slots live.
All inputs are finite; a program needn't handle non-finite values.
Results may differ from the reference program's by a relative error of at most 0.012.
The reference program's roundings to bfloat16 on the way count: a program that leaves them out, or rounds other values in their place, can miss the bound.
Values may be sent and summed in bfloat16 or wider, within the bound.
No kernel may reach another device: no remote copies, remote signals or barrier semaphores. Data moves between devices by JAX's collectives and lax.ppermute only.
A program may use at most 320 MiB of HBM per device.

```python
import math
import jax
import jax.numpy as jnp
from jax import lax

D = 18432
HEADS = 24
HEAD = 256
FF = 9216
CACHE = 1024
ROWS = 16
QUERY = 6144


def draw_cache_keys(key, part):
    key = jax.random.fold_in(key, 11)
    base_key = jax.random.fold_in(key, 0)
    base = jax.random.normal(base_key, (ROWS, CACHE, HEAD), jnp.float32)
    return base.astype(jnp.bfloat16)


def draw_lengths(key, part):
    key = jax.random.fold_in(key, 23)
    length_key, full_key = jax.random.split(key)
    drawn = jax.random.randint(length_key, (ROWS,), CACHE // 8, CACHE + 1)
    chosen = jax.random.randint(full_key, (), 0, ROWS)
    return jnp.where(jnp.arange(ROWS) == chosen, CACHE, drawn).astype(jnp.int32)


def place_ends(values, own_key, least, top_value):
    spot = [jax.random.randint(jax.random.fold_in(own_key, axis), (), 0, length) for axis, length in enumerate(values.shape)]
    longest = values.shape.index(max(values.shape))
    neighbour = spot[:longest] + [(spot[longest] + 1) % values.shape[longest]] + spot[longest + 1:]
    return values.at[tuple(spot)].set(least).at[tuple(neighbour)].set(top_value)


def block_scale(key, shape, cuts, least, largest):
    level, own = 1.0, jax.random.fold_in(key, 6)
    for dim, blocks in cuts:
        heights = jnp.exp(jax.random.uniform(jax.random.fold_in(own, dim), (blocks,), jnp.float32, least / len(cuts), largest / len(cuts)))
        level = level * jnp.repeat(heights, shape[dim] // blocks).reshape([-1 if axis == dim else 1 for axis in range(len(shape))])
    return level


def bell_draw(stream_key, dims, scale, limit, shards=(), kind=jnp.bfloat16):
    entries = scale * jax.random.normal(stream_key, dims, jnp.float32)
    if shards:
        entries = entries * block_scale(stream_key, dims, shards, -0.22, 0.18)
    return jnp.clip(entries, -limit, limit).astype(kind)


def setup_inputs(seed: int = 0, part: int = 0) -> dict:
    key_of = jax.random.split(jax.random.key(seed), 13)
    part_splits = jax.random.split(jax.random.fold_in(key_of[12], part), 13)
    return {
        "tokens": bell_draw(part_splits[0], (2, ROWS, D), 1.0, 6.0, ((1, 16),)),
        "norm_gain": jnp.clip(1.0 + 0.18 * jax.random.normal(key_of[1], (D,), jnp.float32), 0.1, 1.9),
        "w_query": bell_draw(key_of[2], (QUERY, D), D ** -0.5, 0.046875, ((0, 16),)),
        "w_keyval": bell_draw(key_of[3], (2 * HEAD, D), D ** -0.5, 0.046875, ((0, 16),)),
        "w_gate": bell_draw(key_of[4], (FF, D), D ** -0.5, 0.046875, ((0, 16),)),
        "w_up": bell_draw(key_of[5], (FF, D), D ** -0.5, 0.046875, ((0, 16),)),
        "w_out": bell_draw(key_of[6], (QUERY, D), QUERY ** -0.5, 0.078125, ((0, 16),)),
        "w_down": bell_draw(key_of[7], (FF, D), FF ** -0.5, 0.0625, ((0, 16),)),
        "cache_keys": draw_cache_keys(jax.random.fold_in(jax.random.fold_in(key_of[12], part), 71), part),
        "cache_values": bell_draw(part_splits[9], (ROWS, CACHE, HEAD), 1.0, 6.0, ((0, 16),)),
        "lengths": draw_lengths(jax.random.fold_in(jax.random.fold_in(key_of[12], part), 71), part),
        "positions": place_ends(jax.random.randint(part_splits[11], (ROWS,), CACHE, 4 * CACHE), jax.random.fold_in(part_splits[11], 1), CACHE, (4 * CACHE) - 1).astype(jnp.int32),
    }


def layer_norm(tokens, norm_gain):
    values = tokens.astype(jnp.float32)
    center = lax.optimization_barrier(jnp.mean(values, axis=-1, keepdims=True))
    spread = lax.optimization_barrier(jnp.mean((values - center) ** 2, axis=-1, keepdims=True))
    return ((values - center) / jnp.sqrt(spread + 1e-05) * norm_gain).astype(jnp.bfloat16)

def rotate(vector, angle_pos):
    half = vector.shape[-1] // 2
    freq = jnp.exp(-math.log(10000.0) * jnp.arange(half, dtype=jnp.float32) / half)
    angle = angle_pos[..., None] * freq
    first = vector[..., :half]
    second = vector[..., half:]
    return jnp.concatenate([first * jnp.cos(angle) - second * jnp.sin(angle), second * jnp.cos(angle) + first * jnp.sin(angle)], axis=-1)

def attend(queries, extra_keys, extra_values, cache_keys, cache_values, lengths):
    scale = 1.0 / math.sqrt(queries.shape[-1])
    cached = jnp.einsum('rhd,rld->rhl', queries.astype(jnp.float32), cache_keys.astype(jnp.float32)) * scale
    live = jnp.arange(cache_keys.shape[1])[None, None, :] < lengths[:, None, None]
    cached = jnp.where(live, cached, -1e+30)
    fresh = jnp.einsum('rhd,red->rhe', queries.astype(jnp.float32), extra_keys.astype(jnp.float32)) * scale
    top = jnp.maximum(lax.optimization_barrier(jnp.max(cached, axis=-1)), lax.optimization_barrier(jnp.max(fresh, axis=-1)))
    cached_exp = jnp.exp(cached - top[..., None])
    fresh_exp = jnp.exp(fresh - top[..., None])
    total = lax.optimization_barrier(jnp.sum(cached_exp, axis=-1)) + lax.optimization_barrier(jnp.sum(fresh_exp, axis=-1))
    cached_w = (cached_exp / total[..., None]).astype(jnp.bfloat16)
    fresh_w = (fresh_exp / total[..., None]).astype(jnp.bfloat16)
    result = jnp.einsum('rhl,rld->rhd', cached_w.astype(jnp.float32), cache_values.astype(jnp.float32))
    result = result + jnp.einsum('rhe,red->rhd', fresh_w.astype(jnp.float32), extra_values.astype(jnp.float32))
    return result.astype(jnp.bfloat16).reshape(queries.shape[0], -1)

def reference(tokens, norm_gain, w_query, w_keyval, w_gate, w_up, w_out, w_down, cache_keys, cache_values, lengths, positions):
    normed = layer_norm(tokens, norm_gain)
    flat = normed.reshape(2 * ROWS, D)
    query = jnp.dot(flat, w_query.T, preferred_element_type=jnp.float32).reshape(2, ROWS, HEADS, HEAD)
    keyval = jnp.dot(flat, w_keyval.T, preferred_element_type=jnp.float32).reshape(2, ROWS, 2 * HEAD)
    gate = jnp.dot(flat, w_gate.T, preferred_element_type=jnp.float32)
    upward = jnp.dot(flat, w_up.T, preferred_element_type=jnp.float32)
    hidden = (jax.nn.silu(gate) * upward).astype(jnp.bfloat16)
    new_keys = []
    new_values = []
    attended = []
    for offset in range(2):
        angle_pos = (positions + offset).astype(jnp.float32)
        rotated = rotate(query[offset], angle_pos[:, None]).astype(jnp.bfloat16)
        new_keys.append(rotate(keyval[offset, :, :HEAD], angle_pos).astype(jnp.bfloat16))
        new_values.append(keyval[offset, :, HEAD:].astype(jnp.bfloat16))
        attended.append(attend(rotated, jnp.stack(new_keys, axis=1), jnp.stack(new_values, axis=1), cache_keys, cache_values, lengths))
    attended = jnp.stack(attended).reshape(2 * ROWS, HEADS * HEAD)
    branch = jnp.dot(attended, w_out, preferred_element_type=jnp.float32) + jnp.dot(hidden, w_down, preferred_element_type=jnp.float32)
    return (tokens.astype(jnp.float32) + branch.reshape(2, ROWS, D)).astype(jnp.bfloat16)
```

```python
import math

import jax
import jax.numpy as jnp
from jax import lax
from jax.sharding import PartitionSpec as P


def layer_norm(tokens, norm_gain):
    values = tokens.astype(jnp.float32)
    center = jnp.mean(values, axis=-1, keepdims=True)
    spread = jnp.mean((values - center) ** 2, axis=-1, keepdims=True)
    return ((values - center) / jnp.sqrt(spread + 1e-05) * norm_gain).astype(jnp.bfloat16)


def rotate(vector, angle_pos):
    half = vector.shape[-1] // 2
    freq = jnp.exp(-math.log(10000.0) * jnp.arange(half, dtype=jnp.float32) / half)
    angle = angle_pos[..., None] * freq
    first = vector[..., :half]
    second = vector[..., half:]
    return jnp.concatenate(
        [
            first * jnp.cos(angle) - second * jnp.sin(angle),
            second * jnp.cos(angle) + first * jnp.sin(angle),
        ],
        axis=-1,
    )


def attend(queries, new_keys, new_values, cache_keys, cache_values, lengths):
    steps = queries.shape[1]
    scale = 1.0 / math.sqrt(queries.shape[-1])
    cached = (
        jnp.einsum("rthd,rld->rthl", queries, cache_keys, preferred_element_type=jnp.float32)
        * scale
    )
    live = jnp.arange(cache_keys.shape[1])[None, None, None, :] < lengths[:, None, None, None]
    cached = jnp.where(live, cached, -1e30)
    fresh = (
        jnp.einsum("rthd,red->rthe", queries, new_keys, preferred_element_type=jnp.float32) * scale
    )
    known = jnp.arange(steps)[None, :] <= jnp.arange(steps)[:, None]
    fresh = jnp.where(known[None, :, None, :], fresh, -1e30)
    top = jnp.maximum(jnp.max(cached, axis=-1), jnp.max(fresh, axis=-1))
    cached_exp = jnp.exp(cached - top[..., None])
    fresh_exp = jnp.exp(fresh - top[..., None])
    total = jnp.sum(cached_exp, axis=-1) + jnp.sum(fresh_exp, axis=-1)
    cached_w = (cached_exp / total[..., None]).astype(jnp.bfloat16)
    fresh_w = (fresh_exp / total[..., None]).astype(jnp.bfloat16)
    result = jnp.einsum(
        "rthl,rld->rthd", cached_w, cache_values, preferred_element_type=jnp.float32
    )
    result = result + jnp.einsum(
        "rthe,red->rthd", fresh_w, new_values, preferred_element_type=jnp.float32
    )
    return result.astype(jnp.bfloat16)


def local(
    tokens,
    norm_gain,
    w_query,
    w_keyval,
    w_gate,
    w_up,
    w_out,
    w_down,
    cache_keys,
    cache_values,
    lengths,
    positions,
):
    steps, rows, width = tokens.shape
    head = cache_keys.shape[2]
    query_cols = w_query.shape[0]
    devices = lax.axis_size("gx")
    normed = layer_norm(tokens, norm_gain)
    everyone = lax.all_gather(normed, "gx", axis=0, tiled=False).reshape(-1, width)

    def project(weight):
        return jnp.einsum("nd,cd->nc", everyone, weight, preferred_element_type=jnp.float32)

    attention_in = jnp.concatenate([project(w_query), project(w_keyval)], axis=1)
    attention_in = attention_in.reshape(devices, steps * rows, -1)
    arrived = lax.all_to_all(attention_in, "gx", split_axis=0, concat_axis=0, tiled=True)
    arrived = arrived.reshape(devices, steps, rows, -1).transpose(2, 1, 0, 3)
    query = arrived[..., :query_cols].reshape(rows, steps, -1, head)
    keyval = arrived[..., query_cols:].reshape(rows, steps, 2 * head)
    hidden = (jax.nn.silu(project(w_gate)) * project(w_up)).astype(jnp.bfloat16)

    angle_pos = (positions[:, None] + jnp.arange(steps)[None, :]).astype(jnp.float32)
    rotated = rotate(query, angle_pos[:, :, None]).astype(jnp.bfloat16)
    new_keys = rotate(keyval[..., :head], angle_pos).astype(jnp.bfloat16)
    new_values = keyval[..., head:].astype(jnp.bfloat16)
    attended = attend(rotated, new_keys, new_values, cache_keys, cache_values, lengths)
    attended = attended.reshape(rows, steps, devices, -1).transpose(2, 1, 0, 3)
    attended = lax.all_to_all(attended, "gx", split_axis=0, concat_axis=0, tiled=True)
    attended = attended.reshape(devices * steps * rows, -1)

    branch = jnp.dot(attended, w_out, preferred_element_type=jnp.float32)
    branch = branch + jnp.dot(hidden, w_down, preferred_element_type=jnp.float32)
    branch = lax.psum_scatter(
        branch.reshape(devices, steps * rows, width), "gx", scatter_dimension=0, tiled=True
    )
    branch = branch.reshape(steps, rows, width)
    return (tokens.astype(jnp.float32) + branch).astype(jnp.bfloat16)


def solution(mesh):
    in_specs = (
        P(None, ("groups", "gx"), None),
        P(),
        P("gx", None),
        P("gx", None),
        P("gx", None),
        P("gx", None),
        P("gx", None),
        P("gx", None),
        P(("groups", "gx"), None, None),
        P(("groups", "gx"), None, None),
        P(("groups", "gx")),
        P(("groups", "gx")),
    )
    out_specs = P(None, ("groups", "gx"), None)
    return jax.shard_map(local, mesh=mesh, in_specs=in_specs, out_specs=out_specs, check_vma=False)
```

```python
import functools
import math

import jax
import jax.numpy as jnp
from jax import lax
from jax.experimental import pallas as pl
from jax.experimental.pallas import tpu as pltpu
from jax.sharding import PartitionSpec as P

F32 = jnp.float32
BF16 = jnp.bfloat16
NT = (((1,), (1,)), ((), ()))
ANY = pl.BlockSpec(memory_space=pl.ANY)
VMEM = pl.BlockSpec(memory_space=pltpu.VMEM)
SMEM = pl.BlockSpec(memory_space=pltpu.SMEM)


def params(mib):
    return pltpu.CompilerParams(vmem_limit_bytes=mib << 20)


def cost(rows, *weights):
    size = sum(math.prod(w.shape) for w in weights)
    return pl.CostEstimate(flops=2 * rows * size, bytes_accessed=2 * size, transcendentals=0)


def slot_at(place, half):
    return 2 * place if place < half else 2 * (place - half) + 1


def cuts(width):
    for count in (8, 9, 6, 4, 3, 2):
        if width % (128 * count) == 0:
            return count
    return 1


def norm_kernel(tokens_ref, gain_ref, out_ref):
    values = tokens_ref[...].astype(F32)
    centered = values - jnp.mean(values, axis=-1, keepdims=True)
    spread = jnp.mean(centered * centered, axis=-1, keepdims=True)
    out_ref[...] = (centered / jnp.sqrt(spread + 1e-05) * gain_ref[...]).astype(BF16)


def layer_norm(tokens, norm_gain):
    return pl.pallas_call(
        norm_kernel, out_shape=jax.ShapeDtypeStruct(tokens.shape, BF16)
    )(tokens, norm_gain.reshape(1, -1))


def attention_in_kernel(
    chunks, me_ref, mine_ref, other_ref, wq_ref, wk_ref, out_ref, rows_ref,
    pieces, spread, rows, wq, wk, acc_q, acc_k, piece_sem, q_sem, k_sem, rows_sem,
):
    half, steps, width = mine_ref.shape
    step = width // chunks

    def cols(c):
        return pl.ds(c * step, step)

    piece_copies = [
        pltpu.make_async_copy(mine_ref, pieces.at[pl.ds(0, half)], piece_sem.at[0]),
        pltpu.make_async_copy(other_ref, pieces.at[pl.ds(half, half)], piece_sem.at[1]),
    ]
    q_copies = [
        pltpu.make_async_copy(wq_ref.at[:, cols(c)], wq.at[c], q_sem.at[c]) for c in range(chunks)
    ]
    k_copies = [
        pltpu.make_async_copy(wk_ref.at[:, cols(c)], wk.at[c], k_sem.at[c]) for c in range(chunks)
    ]
    row_copies = [
        pltpu.make_async_copy(rows.at[:, cols(c)], rows_ref.at[:, cols(c)], rows_sem.at[c])
        for c in range(chunks)
    ]
    for copy in piece_copies:
        copy.start()
    for c in range(chunks):
        q_copies[c].start()
        k_copies[c].start()
    acc_q[...] = jnp.zeros_like(acc_q)
    acc_k[...] = jnp.zeros_like(acc_k)
    for copy in piece_copies:
        copy.wait()
    for c in range(chunks):
        part = slice(c * step, (c + 1) * step)
        for p in range(2 * half):
            spread[p * steps : (p + 1) * steps, :] = pieces[p, :, part].astype(F32)
        block = spread[...].astype(BF16)
        rows[:, part] = block
        row_copies[c].start()
        q_copies[c].wait()
        acc_q[...] += lax.dot_general(block, wq[c], NT, preferred_element_type=F32)
        k_copies[c].wait()
        acc_k[...] += lax.dot_general(block, wk[c], NT, preferred_element_type=F32)
    split = acc_q.shape[1]
    for p in range(2 * half):
        owner = lax.bitwise_xor(me_ref[0], slot_at(p, half))
        out_ref[owner, :, :split] = acc_q[p * steps : (p + 1) * steps, :]
        out_ref[owner, :, split:] = acc_k[p * steps : (p + 1) * steps, :]
    for copy in row_copies:
        copy.wait()


def attention_in(me, mine, other, w_query, w_keyval):
    half, steps, width = mine.shape
    n = 2 * half * steps
    chunks = cuts(width)
    step = width // chunks
    q_cols, k_cols = w_query.shape[0], w_keyval.shape[0]
    return pl.pallas_call(
        functools.partial(attention_in_kernel, chunks),
        in_specs=[SMEM, ANY, ANY, ANY, ANY],
        out_specs=[VMEM, ANY],
        out_shape=[
            jax.ShapeDtypeStruct((2 * half, steps, q_cols + k_cols), F32),
            jax.ShapeDtypeStruct((n, width), BF16),
        ],
        scratch_shapes=[
            pltpu.VMEM((2 * half, steps, width), BF16),
            pltpu.VMEM((n, step), F32),
            pltpu.VMEM((n, width), BF16),
            pltpu.VMEM((chunks, q_cols, step), BF16),
            pltpu.VMEM((chunks, k_cols, step), BF16),
            pltpu.VMEM((n, q_cols), F32),
            pltpu.VMEM((n, k_cols), F32),
            pltpu.SemaphoreType.DMA((2,)),
            pltpu.SemaphoreType.DMA((chunks,)),
            pltpu.SemaphoreType.DMA((chunks,)),
            pltpu.SemaphoreType.DMA((chunks,)),
        ],
        compiler_params=params(52),
        cost_estimate=cost(n, w_query, w_keyval),
    )(me, mine, other, w_query, w_keyval)


def hidden_kernel(
    chunks, rows_ref, wg_ref, wu_ref, out_ref, rows, wg, wu, acc_g, acc_u, row_sem, g_sem, u_sem
):
    step = rows_ref.shape[1] // chunks

    def cols(c):
        return pl.ds(c * step, step)

    row_copy = pltpu.make_async_copy(rows_ref, rows, row_sem)
    copies = [
        (
            pltpu.make_async_copy(wg_ref.at[:, cols(c)], wg.at[c], g_sem.at[c]),
            pltpu.make_async_copy(wu_ref.at[:, cols(c)], wu.at[c], u_sem.at[c]),
        )
        for c in range(chunks)
    ]
    row_copy.start()
    for gate_copy, up_copy in copies:
        gate_copy.start()
        up_copy.start()
    acc_g[...] = jnp.zeros_like(acc_g)
    acc_u[...] = jnp.zeros_like(acc_u)
    row_copy.wait()
    for c in range(chunks):
        block = rows[:, c * step : (c + 1) * step]
        copies[c][0].wait()
        acc_g[...] += lax.dot_general(block, wg[c], NT, preferred_element_type=F32)
        copies[c][1].wait()
        acc_u[...] += lax.dot_general(block, wu[c], NT, preferred_element_type=F32)
    gate = acc_g[...]
    out_ref[...] = (jax.nn.silu(gate) * acc_u[...]).astype(BF16)


def hidden_units(rows, w_gate, w_up):
    n, width = rows.shape
    units = w_gate.shape[0]
    chunks = cuts(width)
    step = width // chunks
    return pl.pallas_call(
        functools.partial(hidden_kernel, chunks),
        in_specs=[ANY, ANY, ANY],
        out_specs=VMEM,
        out_shape=jax.ShapeDtypeStruct((n, units), BF16),
        scratch_shapes=[
            pltpu.VMEM((n, width), BF16),
            pltpu.VMEM((chunks, units, step), BF16),
            pltpu.VMEM((chunks, units, step), BF16),
            pltpu.VMEM((n, units), F32),
            pltpu.VMEM((n, units), F32),
            pltpu.SemaphoreType.DMA,
            pltpu.SemaphoreType.DMA((chunks,)),
            pltpu.SemaphoreType.DMA((chunks,)),
        ],
        compiler_params=params(56),
        cost_estimate=cost(n, w_gate, w_up),
    )(rows, w_gate, w_up)


def down_kernel(chunks, hidden_ref, w_ref, out_ref, w, out, w_sem, out_sem):
    step = w_ref.shape[1] // chunks

    def cols(c):
        return pl.ds(c * step, step)

    copies = [
        pltpu.make_async_copy(w_ref.at[:, cols(c)], w.at[c], w_sem.at[c]) for c in range(chunks)
    ]
    out_copies = [
        pltpu.make_async_copy(out.at[c], out_ref.at[:, cols(c)], out_sem.at[c])
        for c in range(chunks)
    ]
    for copy in copies:
        copy.start()
    for c in range(chunks):
        copies[c].wait()
        out[c] = jnp.dot(hidden_ref[...], w[c], preferred_element_type=F32)
        out_copies[c].start()
    for copy in out_copies:
        copy.wait()


def down_part(hidden, w_down):
    n, units = hidden.shape
    width = w_down.shape[1]
    chunks = cuts(width)
    step = width // chunks
    return pl.pallas_call(
        functools.partial(down_kernel, chunks),
        in_specs=[VMEM, ANY],
        out_specs=ANY,
        out_shape=jax.ShapeDtypeStruct((n, width), F32),
        scratch_shapes=[
            pltpu.VMEM((chunks, units, step), BF16),
            pltpu.VMEM((chunks, n, step), F32),
            pltpu.SemaphoreType.DMA((chunks,)),
            pltpu.SemaphoreType.DMA((chunks,)),
        ],
        compiler_params=params(40),
        cost_estimate=cost(n, w_down),
    )(hidden, w_down)


def branch_kernel(
    chunks, me_ref, attended_ref, part_ref, w_ref, keep_ref, send_ref,
    spread, w, part, keep, send, w_sem, part_sem, keep_sem, send_sem,
):
    slots, steps, _ = attended_ref.shape
    half = keep_ref.shape[0]
    step = w_ref.shape[1] // chunks

    def cols(c):
        return pl.ds(c * step, step)

    copies = [
        (
            pltpu.make_async_copy(w_ref.at[:, cols(c)], w.at[c], w_sem.at[c]),
            pltpu.make_async_copy(part_ref.at[:, cols(c)], part.at[c], part_sem.at[c]),
        )
        for c in range(chunks)
    ]
    out_copies = [
        (
            pltpu.make_async_copy(keep.at[c], keep_ref.at[:, cols(c)], keep_sem.at[c]),
            pltpu.make_async_copy(send.at[c], send_ref.at[:, cols(c)], send_sem.at[c]),
        )
        for c in range(chunks)
    ]
    for w_copy, part_copy in copies:
        w_copy.start()
        part_copy.start()
    for p in range(slots):
        owner = lax.bitwise_xor(me_ref[0], slot_at(p, slots // 2))
        spread[p * steps : (p + 1) * steps, :] = attended_ref[owner].astype(F32)
    attended = spread[...].astype(BF16)
    for c in range(chunks):
        for copy in copies[c]:
            copy.wait()
        total = part[c] + jnp.dot(attended, w[c], preferred_element_type=F32)
        keep[c] = total[:half]
        send[c] = total[half:].astype(BF16)
        for copy in out_copies[c]:
            copy.start()
    for pair in out_copies:
        for copy in pair:
            copy.wait()


def branch_parts(me, attended, part, w_out):
    slots, steps, features = attended.shape
    n, width = part.shape
    half = n // 2
    chunks = cuts(width)
    step = width // chunks
    return pl.pallas_call(
        functools.partial(branch_kernel, chunks),
        in_specs=[SMEM, VMEM, ANY, ANY],
        out_specs=[ANY, ANY],
        out_shape=[
            jax.ShapeDtypeStruct((half, width), F32),
            jax.ShapeDtypeStruct((half, width), BF16),
        ],
        scratch_shapes=[
            pltpu.VMEM((n, features), F32),
            pltpu.VMEM((chunks, features, step), BF16),
            pltpu.VMEM((chunks, n, step), F32),
            pltpu.VMEM((chunks, half, step), F32),
            pltpu.VMEM((chunks, half, step), BF16),
            pltpu.SemaphoreType.DMA((chunks,)),
            pltpu.SemaphoreType.DMA((chunks,)),
            pltpu.SemaphoreType.DMA((chunks,)),
            pltpu.SemaphoreType.DMA((chunks,)),
        ],
        compiler_params=params(40),
        cost_estimate=cost(n, w_out),
    )(me, attended, part, w_out)


def cut_kernel(keep_ref, came_ref, own_ref, *send_refs):
    steps = own_ref.shape[0]
    total = keep_ref[...] + came_ref[...].astype(F32)
    own_ref[...] = total[:steps]
    for p, send_ref in enumerate(send_refs):
        send_ref[...] = total[(p + 1) * steps : (p + 2) * steps].astype(BF16)


def cut_parts(keep, came, steps):
    half, width = keep.shape
    slots = half // steps
    chunks = 3 if width % 384 == 0 else 1
    step = width // chunks
    whole = pl.BlockSpec((half, step), lambda c: (0, c))
    piece = pl.BlockSpec((steps, step), lambda c: (0, c))
    return pl.pallas_call(
        cut_kernel,
        grid=(chunks,),
        in_specs=[whole, whole],
        out_specs=[piece] * slots,
        out_shape=[jax.ShapeDtypeStruct((steps, width), F32)]
        + [jax.ShapeDtypeStruct((steps, width), BF16)] * (slots - 1),
        compiler_params=params(32),
        cost_estimate=pl.CostEstimate(
            flops=2 * half * width, bytes_accessed=8 * half * width, transcendentals=0
        ),
    )(keep, came)


def rotate(vector, angle_pos):
    half = vector.shape[-1] // 2
    freq = jnp.exp(-math.log(10000.0) * jnp.arange(half, dtype=F32) / half)
    angle = angle_pos[..., None] * freq
    first = vector[..., :half]
    second = vector[..., half:]
    return jnp.concatenate(
        [
            first * jnp.cos(angle) - second * jnp.sin(angle),
            second * jnp.cos(angle) + first * jnp.sin(angle),
        ],
        axis=-1,
    )


def attend(queries, new_keys, new_values, cache_keys, cache_values, lengths):
    steps = queries.shape[1]
    scale = 1.0 / math.sqrt(queries.shape[-1])
    cached = jnp.einsum("rthd,rld->rthl", queries, cache_keys, preferred_element_type=F32) * scale
    live = jnp.arange(cache_keys.shape[1])[None, None, None, :] < lengths[:, None, None, None]
    cached = jnp.where(live, cached, -1e30)
    fresh = jnp.einsum("rthd,red->rthe", queries, new_keys, preferred_element_type=F32) * scale
    known = jnp.arange(steps)[None, :] <= jnp.arange(steps)[:, None]
    fresh = jnp.where(known[None, :, None, :], fresh, -1e30)
    top = jnp.maximum(jnp.max(cached, axis=-1), jnp.max(fresh, axis=-1))
    cached_exp = jnp.exp(cached - top[..., None])
    fresh_exp = jnp.exp(fresh - top[..., None])
    total = jnp.sum(cached_exp, axis=-1) + jnp.sum(fresh_exp, axis=-1)
    cached_w = (cached_exp / total[..., None]).astype(BF16)
    fresh_w = (fresh_exp / total[..., None]).astype(BF16)
    result = jnp.einsum("rthl,rld->rthd", cached_w, cache_values, preferred_element_type=F32)
    result = result + jnp.einsum("rthe,red->rthd", fresh_w, new_values, preferred_element_type=F32)
    return result.astype(BF16)


def swap(value, bits, devices):
    return lax.ppermute(value, "gx", [(i, i ^ bits) for i in range(devices)])


def gather_rows(piece, devices):
    outer = min(4, devices // 2)
    inner = devices // (2 * outer)
    near = [piece] + [swap(piece, 2 * inner * a, devices) for a in range(1, outer)]
    far = [near] + [[swap(p, 2 * b, devices) for p in near] for b in range(1, inner)]
    even = jnp.stack([far[b][a] for a in range(outer) for b in range(inner)])
    return even, swap(even, 1, devices)


def local(
    tokens,
    norm_gain,
    w_query,
    w_keyval,
    w_gate,
    w_up,
    w_out,
    w_down,
    cache_keys,
    cache_values,
    lengths,
    positions,
):
    steps, rows, width = tokens.shape
    head = cache_keys.shape[2]
    query_cols = w_query.shape[0]
    devices = lax.axis_size("gx")
    batch = steps * rows
    me = lax.axis_index("gx").astype(jnp.int32).reshape(1)

    own_tokens = tokens.reshape(batch, width)
    even, odd = gather_rows(layer_norm(own_tokens, norm_gain), devices)
    projected, everyone = attention_in(me, even, odd, w_query, w_keyval)

    arrived = lax.all_to_all(projected, "gx", split_axis=0, concat_axis=0, tiled=True)
    arrived = arrived.reshape(devices, steps, rows, -1).transpose(2, 1, 0, 3)
    query = arrived[..., :query_cols].reshape(rows, steps, -1, head)
    keyval = arrived[..., query_cols:].reshape(rows, steps, 2 * head)
    hidden = hidden_units(everyone, w_gate, w_up)

    angle_pos = (positions[:, None] + jnp.arange(steps)[None, :]).astype(F32)
    rotated = rotate(query, angle_pos[:, :, None]).astype(BF16)
    new_keys = rotate(keyval[..., :head], angle_pos).astype(BF16)
    new_values = keyval[..., head:].astype(BF16)
    attended = attend(rotated, new_keys, new_values, cache_keys, cache_values, lengths)
    attended = attended.reshape(rows, steps, devices, -1).transpose(2, 1, 0, 3)
    attended = attended.reshape(devices, batch, -1)
    attended = lax.all_to_all(attended, "gx", split_axis=0, concat_axis=0, tiled=True)

    part = down_part(hidden, w_down)
    keep, send = branch_parts(me, attended, part, w_out)
    pieces = cut_parts(keep, swap(send, 1, devices), batch)
    branch = pieces[0]
    for place in range(1, devices // 2):
        branch = branch + swap(pieces[place], 2 * place, devices).astype(F32)
    result = (own_tokens.astype(F32) + branch).astype(BF16)
    return result.reshape(tokens.shape)


def solution(mesh):
    in_specs = (
        P(None, ("groups", "gx"), None),
        P(),
        P("gx", None),
        P("gx", None),
        P("gx", None),
        P("gx", None),
        P("gx", None),
        P("gx", None),
        P(("groups", "gx"), None, None),
        P(("groups", "gx"), None, None),
        P(("groups", "gx")),
        P(("groups", "gx")),
    )
    out_specs = P(None, ("groups", "gx"), None)
    return jax.shard_map(local, mesh=mesh, in_specs=in_specs, out_specs=out_specs, check_vma=False)
```

```python
import functools
import math

import jax
import jax.numpy as jnp
from jax import lax
from jax.experimental import pallas as pl
from jax.experimental.pallas import tpu as pltpu
from jax.sharding import PartitionSpec as P

F32 = jnp.float32
BF16 = jnp.bfloat16
NT = (((1,), (1,)), ((), ()))
ANY = pl.BlockSpec(memory_space=pl.ANY)
VMEM = pl.BlockSpec(memory_space=pltpu.VMEM)
SMEM = pl.BlockSpec(memory_space=pltpu.SMEM)


def params(mib):
    return pltpu.CompilerParams(vmem_limit_bytes=mib << 20)


def cost(rows, *weights):
    size = sum(math.prod(w.shape) for w in weights)
    return pl.CostEstimate(flops=2 * rows * size, bytes_accessed=2 * size, transcendentals=0)


def slot_at(place, half):
    return 2 * place if place < half else 2 * (place - half) + 1


def cuts(width):
    for count in (8, 9, 6, 4, 3, 2):
        if width % (128 * count) == 0:
            return count
    return 1


def norm_kernel(tokens_ref, gain_ref, out_ref):
    values = tokens_ref[...].astype(F32)
    centered = values - jnp.mean(values, axis=-1, keepdims=True)
    spread = jnp.mean(centered * centered, axis=-1, keepdims=True)
    out_ref[...] = (centered / jnp.sqrt(spread + 1e-05) * gain_ref[...]).astype(BF16)


def layer_norm(tokens, norm_gain):
    return pl.pallas_call(
        norm_kernel, out_shape=jax.ShapeDtypeStruct(tokens.shape, BF16)
    )(tokens, norm_gain.reshape(1, -1))


def attention_in_kernel(
    chunks, groups, me_ref, even_ref, odd_ref, wq_ref, wk_ref, out_ref, rows_ref,
    spread, rows, acc, q_sem, k_sem, rows_sem, *weights,
):
    half, steps, width = even_ref.shape
    step = width // chunks
    split = wq_ref.shape[0]

    def cols(c):
        return pl.ds(c * step, step)

    def place(c, which):
        if groups == 2:
            return weights[which].at[c]
        return weights[0].at[c, pl.ds(which * split, (wq_ref, wk_ref)[which].shape[0])]

    copies = [
        (
            pltpu.make_async_copy(wq_ref.at[:, cols(c)], place(c, 0), q_sem.at[c]),
            pltpu.make_async_copy(wk_ref.at[:, cols(c)], place(c, 1), k_sem.at[c]),
        )
        for c in range(chunks)
    ]
    row_copies = [
        pltpu.make_async_copy(rows.at[:, cols(c)], rows_ref.at[:, cols(c)], rows_sem.at[c])
        for c in range(chunks)
    ]
    for pair in copies:
        for copy in pair:
            copy.start()
    acc[...] = jnp.zeros_like(acc)
    for c in range(chunks):
        part = slice(c * step, (c + 1) * step)
        for p in range(half):
            spread[p * steps : (p + 1) * steps, :] = even_ref[p, :, part].astype(F32)
            q = half + p
            spread[q * steps : (q + 1) * steps, :] = odd_ref[p, :, part].astype(F32)
        block = spread[...].astype(BF16)
        rows[:, part] = block
        row_copies[c].start()
        for copy in copies[c]:
            copy.wait()
        first = 0
        for weight in weights:
            last = first + weight.shape[1]
            acc[:, first:last] += lax.dot_general(
                block, weight[c], NT, preferred_element_type=F32
            )
            first = last
    for p in range(2 * half):
        owner = lax.bitwise_xor(me_ref[0], slot_at(p, half))
        out_ref[owner] = acc[p * steps : (p + 1) * steps, :]
    for copy in row_copies:
        copy.wait()


def attention_in(me, even, odd, w_query, w_keyval):
    half, steps, width = even.shape
    n = 2 * half * steps
    chunks = cuts(width)
    step = width // chunks
    q_cols, k_cols = w_query.shape[0], w_keyval.shape[0]
    groups = 1 if q_cols % 16 == 0 and k_cols % 16 == 0 else 2
    sizes = [q_cols + k_cols] if groups == 1 else [q_cols, k_cols]
    return pl.pallas_call(
        functools.partial(attention_in_kernel, chunks, groups),
        in_specs=[SMEM, VMEM, VMEM, ANY, ANY],
        out_specs=[VMEM, ANY],
        out_shape=[
            jax.ShapeDtypeStruct((2 * half, steps, q_cols + k_cols), F32),
            jax.ShapeDtypeStruct((n, width), BF16),
        ],
        scratch_shapes=[
            pltpu.VMEM((n, step), F32),
            pltpu.VMEM((n, width), BF16),
            pltpu.VMEM((n, q_cols + k_cols), F32),
            pltpu.SemaphoreType.DMA((chunks,)),
            pltpu.SemaphoreType.DMA((chunks,)),
            pltpu.SemaphoreType.DMA((chunks,)),
        ]
        + [pltpu.VMEM((chunks, size, step), BF16) for size in sizes],
        compiler_params=params(52),
        cost_estimate=cost(n, w_query, w_keyval),
    )(me, even, odd, w_query, w_keyval)


def hidden_kernel(
    chunks, rows_ref, wg_ref, wu_ref, out_ref, wg, wu, acc_g, acc_u, g_sem, u_sem
):
    step = rows_ref.shape[1] // chunks

    def cols(c):
        return pl.ds(c * step, step)

    copies = [
        (
            pltpu.make_async_copy(wg_ref.at[:, cols(c)], wg.at[c], g_sem.at[c]),
            pltpu.make_async_copy(wu_ref.at[:, cols(c)], wu.at[c], u_sem.at[c]),
        )
        for c in range(chunks)
    ]
    for gate_copy, up_copy in copies:
        gate_copy.start()
        up_copy.start()
    acc_g[...] = jnp.zeros_like(acc_g)
    acc_u[...] = jnp.zeros_like(acc_u)
    for c in range(chunks):
        block = rows_ref[:, c * step : (c + 1) * step]
        copies[c][0].wait()
        acc_g[...] += lax.dot_general(block, wg[c], NT, preferred_element_type=F32)
        copies[c][1].wait()
        acc_u[...] += lax.dot_general(block, wu[c], NT, preferred_element_type=F32)
    gate = acc_g[...]
    out_ref[...] = (jax.nn.silu(gate) * acc_u[...]).astype(BF16)


def hidden_units(rows, w_gate, w_up):
    n, width = rows.shape
    units = w_gate.shape[0]
    chunks = cuts(width)
    step = width // chunks
    return pl.pallas_call(
        functools.partial(hidden_kernel, chunks),
        in_specs=[VMEM, ANY, ANY],
        out_specs=VMEM,
        out_shape=jax.ShapeDtypeStruct((n, units), BF16),
        scratch_shapes=[
            pltpu.VMEM((chunks, units, step), BF16),
            pltpu.VMEM((chunks, units, step), BF16),
            pltpu.VMEM((n, units), F32),
            pltpu.VMEM((n, units), F32),
            pltpu.SemaphoreType.DMA((chunks,)),
            pltpu.SemaphoreType.DMA((chunks,)),
        ],
        compiler_params=params(56),
        cost_estimate=cost(n, w_gate, w_up),
    )(rows, w_gate, w_up)


def down_kernel(chunks, hidden_ref, w_ref, out_ref, w, out, w_sem, out_sem):
    step = w_ref.shape[1] // chunks

    def cols(c):
        return pl.ds(c * step, step)

    copies = [
        pltpu.make_async_copy(w_ref.at[:, cols(c)], w.at[c], w_sem.at[c]) for c in range(chunks)
    ]
    out_copies = [
        pltpu.make_async_copy(out.at[c], out_ref.at[:, cols(c)], out_sem.at[c])
        for c in range(chunks)
    ]
    for copy in copies:
        copy.start()
    for c in range(chunks):
        copies[c].wait()
        out[c] = jnp.dot(hidden_ref[...], w[c], preferred_element_type=F32)
        out_copies[c].start()
    for copy in out_copies:
        copy.wait()


def down_part(hidden, w_down):
    n, units = hidden.shape
    width = w_down.shape[1]
    chunks = cuts(width)
    step = width // chunks
    return pl.pallas_call(
        functools.partial(down_kernel, chunks),
        in_specs=[VMEM, ANY],
        out_specs=ANY,
        out_shape=jax.ShapeDtypeStruct((n, width), F32),
        scratch_shapes=[
            pltpu.VMEM((chunks, units, step), BF16),
            pltpu.VMEM((chunks, n, step), F32),
            pltpu.SemaphoreType.DMA((chunks,)),
            pltpu.SemaphoreType.DMA((chunks,)),
        ],
        compiler_params=params(40),
        cost_estimate=cost(n, w_down),
    )(hidden, w_down)


def branch_kernel(
    chunks, me_ref, attended_ref, part_ref, w_ref, keep_ref, send_ref,
    spread, w, part, keep, send, w_sem, part_sem, keep_sem, send_sem,
):
    slots, steps, _ = attended_ref.shape
    half = keep_ref.shape[0]
    step = w_ref.shape[1] // chunks

    def cols(c):
        return pl.ds(c * step, step)

    copies = [
        (
            pltpu.make_async_copy(w_ref.at[:, cols(c)], w.at[c], w_sem.at[c]),
            pltpu.make_async_copy(part_ref.at[:, cols(c)], part.at[c], part_sem.at[c]),
        )
        for c in range(chunks)
    ]
    out_copies = [
        (
            pltpu.make_async_copy(keep.at[c], keep_ref.at[:, cols(c)], keep_sem.at[c]),
            pltpu.make_async_copy(send.at[c], send_ref.at[:, cols(c)], send_sem.at[c]),
        )
        for c in range(chunks)
    ]
    for w_copy, part_copy in copies:
        w_copy.start()
        part_copy.start()
    for p in range(slots):
        owner = lax.bitwise_xor(me_ref[0], slot_at(p, slots // 2))
        spread[p * steps : (p + 1) * steps, :] = attended_ref[owner].astype(F32)
    attended = spread[...].astype(BF16)
    for c in range(chunks):
        for copy in copies[c]:
            copy.wait()
        total = part[c] + jnp.dot(attended, w[c], preferred_element_type=F32)
        keep[c] = total[:half]
        send[c] = total[half:].astype(BF16)
        for copy in out_copies[c]:
            copy.start()
    for pair in out_copies:
        for copy in pair:
            copy.wait()


def branch_parts(me, attended, part, w_out):
    slots, steps, features = attended.shape
    n, width = part.shape
    half = n // 2
    chunks = cuts(width)
    step = width // chunks
    return pl.pallas_call(
        functools.partial(branch_kernel, chunks),
        in_specs=[SMEM, VMEM, ANY, ANY],
        out_specs=[ANY, ANY],
        out_shape=[
            jax.ShapeDtypeStruct((half, width), F32),
            jax.ShapeDtypeStruct((half, width), BF16),
        ],
        scratch_shapes=[
            pltpu.VMEM((n, features), F32),
            pltpu.VMEM((chunks, features, step), BF16),
            pltpu.VMEM((chunks, n, step), F32),
            pltpu.VMEM((chunks, half, step), F32),
            pltpu.VMEM((chunks, half, step), BF16),
            pltpu.SemaphoreType.DMA((chunks,)),
            pltpu.SemaphoreType.DMA((chunks,)),
            pltpu.SemaphoreType.DMA((chunks,)),
            pltpu.SemaphoreType.DMA((chunks,)),
        ],
        compiler_params=params(40),
        cost_estimate=cost(n, w_out),
    )(me, attended, part, w_out)


def cut_kernel(keep_ref, came_ref, own_ref, *send_refs):
    steps = own_ref.shape[0]
    total = keep_ref[...] + came_ref[...].astype(F32)
    own_ref[...] = total[:steps]
    for p, send_ref in enumerate(send_refs):
        send_ref[...] = total[(p + 1) * steps : (p + 2) * steps].astype(BF16)


def cut_parts(keep, came, steps):
    half, width = keep.shape
    slots = half // steps
    chunks = 3 if width % 384 == 0 else 1
    step = width // chunks
    whole = pl.BlockSpec((half, step), lambda c: (0, c))
    piece = pl.BlockSpec((steps, step), lambda c: (0, c))
    return pl.pallas_call(
        cut_kernel,
        grid=(chunks,),
        in_specs=[whole, whole],
        out_specs=[piece] * slots,
        out_shape=[jax.ShapeDtypeStruct((steps, width), F32)]
        + [jax.ShapeDtypeStruct((steps, width), BF16)] * (slots - 1),
        compiler_params=params(32),
        cost_estimate=pl.CostEstimate(
            flops=2 * half * width, bytes_accessed=8 * half * width, transcendentals=0
        ),
    )(keep, came)


def rotate(vector, angle_pos):
    half = vector.shape[-1] // 2
    freq = jnp.exp(-math.log(10000.0) * jnp.arange(half, dtype=F32) / half)
    angle = angle_pos[..., None] * freq
    first = vector[..., :half]
    second = vector[..., half:]
    return jnp.concatenate(
        [
            first * jnp.cos(angle) - second * jnp.sin(angle),
            second * jnp.cos(angle) + first * jnp.sin(angle),
        ],
        axis=-1,
    )


def attend(queries, new_keys, new_values, cache_keys, cache_values, lengths):
    steps = queries.shape[1]
    scale = 1.0 / math.sqrt(queries.shape[-1])
    cached = jnp.einsum("rthd,rld->rthl", queries, cache_keys, preferred_element_type=F32) * scale
    live = jnp.arange(cache_keys.shape[1])[None, None, None, :] < lengths[:, None, None, None]
    cached = jnp.where(live, cached, -1e30)
    fresh = jnp.einsum("rthd,red->rthe", queries, new_keys, preferred_element_type=F32) * scale
    known = jnp.arange(steps)[None, :] <= jnp.arange(steps)[:, None]
    fresh = jnp.where(known[None, :, None, :], fresh, -1e30)
    top = jnp.maximum(jnp.max(cached, axis=-1), jnp.max(fresh, axis=-1))
    cached_exp = jnp.exp(cached - top[..., None])
    fresh_exp = jnp.exp(fresh - top[..., None])
    total = jnp.sum(cached_exp, axis=-1) + jnp.sum(fresh_exp, axis=-1)
    cached_w = (cached_exp / total[..., None]).astype(BF16)
    fresh_w = (fresh_exp / total[..., None]).astype(BF16)
    result = jnp.einsum("rthl,rld->rthd", cached_w, cache_values, preferred_element_type=F32)
    result = result + jnp.einsum("rthe,red->rthd", fresh_w, new_values, preferred_element_type=F32)
    return result.astype(BF16)


def swap(value, bits, devices):
    return lax.ppermute(value, "gx", [(i, i ^ bits) for i in range(devices)])


def gather_rows(piece, devices):
    outer = min(4, devices // 2)
    inner = devices // (2 * outer)
    near = [piece] + [swap(piece, 2 * inner * a, devices) for a in range(1, outer)]
    far = [near] + [[swap(p, 2 * b, devices) for p in near] for b in range(1, inner)]
    even = jnp.stack([far[b][a] for a in range(outer) for b in range(inner)])
    return even, swap(even, 1, devices)


def local(
    tokens,
    norm_gain,
    w_query,
    w_keyval,
    w_gate,
    w_up,
    w_out,
    w_down,
    cache_keys,
    cache_values,
    lengths,
    positions,
):
    steps, rows, width = tokens.shape
    head = cache_keys.shape[2]
    query_cols = w_query.shape[0]
    devices = lax.axis_size("gx")
    batch = steps * rows
    me = lax.axis_index("gx").astype(jnp.int32).reshape(1)

    own_tokens = tokens.reshape(batch, width)
    even, odd = gather_rows(layer_norm(own_tokens, norm_gain), devices)
    projected, everyone = attention_in(me, even, odd, w_query, w_keyval)

    arrived = lax.all_to_all(projected, "gx", split_axis=0, concat_axis=0, tiled=True)
    arrived = arrived.reshape(devices, steps, rows, -1).transpose(2, 1, 0, 3)
    query = arrived[..., :query_cols].reshape(rows, steps, -1, head)
    keyval = arrived[..., query_cols:].reshape(rows, steps, 2 * head)
    hidden = hidden_units(everyone, w_gate, w_up)

    angle_pos = (positions[:, None] + jnp.arange(steps)[None, :]).astype(F32)
    rotated = rotate(query, angle_pos[:, :, None]).astype(BF16)
    new_keys = rotate(keyval[..., :head], angle_pos).astype(BF16)
    new_values = keyval[..., head:].astype(BF16)
    attended = attend(rotated, new_keys, new_values, cache_keys, cache_values, lengths)
    attended = attended.reshape(rows, steps, devices, -1).transpose(2, 1, 0, 3)
    attended = attended.reshape(devices, batch, -1)
    attended = lax.all_to_all(attended, "gx", split_axis=0, concat_axis=0, tiled=True)

    part = down_part(hidden, w_down)
    keep, send = branch_parts(me, attended, part, w_out)
    pieces = cut_parts(keep, swap(send, 1, devices), batch)
    branch = pieces[0]
    for place in range(1, devices // 2):
        branch = branch + swap(pieces[place], 2 * place, devices).astype(F32)
    result = (own_tokens.astype(F32) + branch).astype(BF16)
    return result.reshape(tokens.shape)


def solution(mesh):
    in_specs = (
        P(None, ("groups", "gx"), None),
        P(),
        P("gx", None),
        P("gx", None),
        P("gx", None),
        P("gx", None),
        P("gx", None),
        P("gx", None),
        P(("groups", "gx"), None, None),
        P(("groups", "gx"), None, None),
        P(("groups", "gx")),
        P(("groups", "gx")),
    )
    out_specs = P(None, ("groups", "gx"), None)
    return jax.shard_map(local, mesh=mesh, in_specs=in_specs, out_specs=out_specs, check_vma=False)
```

```python
import functools
import math

import jax
import jax.numpy as jnp
from jax import lax
from jax.experimental import pallas as pl
from jax.experimental.pallas import tpu as pltpu
from jax.sharding import PartitionSpec as P

F32 = jnp.float32
BF16 = jnp.bfloat16
NT = (((1,), (1,)), ((), ()))
ANY = pl.BlockSpec(memory_space=pl.ANY)
VMEM = pl.BlockSpec(memory_space=pltpu.VMEM)


def params(mib):
    return pltpu.CompilerParams(vmem_limit_bytes=mib << 20)


def cost(rows, *weights):
    size = sum(math.prod(w.shape) for w in weights)
    return pl.CostEstimate(flops=2 * rows * size, bytes_accessed=2 * size, transcendentals=0)


def slot_at(place, half):
    return 2 * place if place < half else 2 * (place - half) + 1


def cuts(width):
    for count in (8, 9, 6, 4, 3, 2):
        if width % (128 * count) == 0:
            return count
    return 1


def norm_kernel(tokens_ref, gain_ref, out_ref):
    values = tokens_ref[...].astype(F32)
    centered = values - jnp.mean(values, axis=-1, keepdims=True)
    spread = jnp.mean(centered * centered, axis=-1, keepdims=True)
    out_ref[...] = (centered / jnp.sqrt(spread + 1e-05) * gain_ref[...]).astype(BF16)


def layer_norm(tokens, norm_gain):
    return pl.pallas_call(
        norm_kernel,
        out_shape=jax.ShapeDtypeStruct(tokens.shape, BF16),
        compiler_params=params(4),
        cost_estimate=pl.CostEstimate(
            flops=25 * 10**9, bytes_accessed=75 * 10**6, transcendentals=0
        ),
    )(tokens, norm_gain.reshape(1, -1))


def project_kernel(
    chunks, even_ref, odd_ref, wq_ref, wg_ref, wu_ref, wk_ref, out_ref, hidden_ref,
    spread, rows, acc, sem_u, sem_k, *streams,
):
    half, steps, width = even_ref.shape
    step = width // chunks
    units = wu_ref.shape[0]
    q_cols = wq_ref.shape[0]

    def cols(c):
        return pl.ds(c * step, step)

    slots = streams[0].shape[0]

    def keyval_place(c):
        if len(streams) == 2:
            return streams[1].at[c % slots]
        return streams[0].at[c % slots, pl.ds(units, wk_ref.shape[0])]

    def up_place(c):
        if len(streams) == 2:
            return streams[0].at[c % slots]
        return streams[0].at[c % slots, pl.ds(0, units)]

    copies = [
        (
            pltpu.make_async_copy(wu_ref.at[:, cols(c)], up_place(c), sem_u.at[c]),
            pltpu.make_async_copy(wk_ref.at[:, cols(c)], keyval_place(c), sem_k.at[c]),
        )
        for c in range(chunks)
    ]
    for pair in copies[:slots]:
        for copy in pair:
            copy.start()
    acc[...] = jnp.zeros_like(acc)
    query = jnp.zeros((rows.shape[0], q_cols), F32)
    gate = jnp.zeros((rows.shape[0], units), F32)
    for c in range(chunks):
        part = slice(c * step, (c + 1) * step)
        for p in range(half):
            spread[p * steps : (p + 1) * steps, :] = even_ref[p, :, part].astype(F32)
            q = half + p
            spread[q * steps : (q + 1) * steps, :] = odd_ref[p, :, part].astype(F32)
        block = spread[...].astype(BF16)
        rows[:, part] = block
        query += lax.dot_general(block, wq_ref[:, part], NT, preferred_element_type=F32)
        gate += lax.dot_general(block, wg_ref[:, part], NT, preferred_element_type=F32)
    for c in range(chunks):
        for copy in copies[c]:
            copy.wait()
        first = 0
        for stream in streams:
            last = first + stream.shape[1]
            acc[:, first:last] += lax.dot_general(
                rows[:, c * step : (c + 1) * step], stream[c % slots], NT, preferred_element_type=F32
            )
            first = last
        if c + slots < chunks:
            for copy in copies[c + slots]:
                copy.start()
    me = lax.axis_index("gx")
    for p in range(2 * half):
        owner = lax.bitwise_xor(me, slot_at(p, half))
        out_ref[owner, :, :q_cols] = query[p * steps : (p + 1) * steps]
        out_ref[owner, :, q_cols:] = acc[p * steps : (p + 1) * steps, units:]
    hidden_ref[...] = (jax.nn.silu(gate) * acc[:, :units]).astype(BF16)


def project(even, odd, w_query, w_keyval, w_gate, w_up):
    half, steps, width = even.shape
    n = 2 * half * steps
    chunks = cuts(width)
    step = width // chunks
    q_cols, k_cols, units = w_query.shape[0], w_keyval.shape[0], w_up.shape[0]
    together = k_cols % 16 == 0 and units % 16 == 0
    sizes = [units + k_cols] if together else [units, k_cols]
    slots = min(chunks, 4)
    taken = 2 * slots * step * (units + k_cols) + 6 * n * width + 4 * n * (step + 4 * units)
    near = 2 * width * (q_cols + units)
    taken += near if near < 8 << 20 else 0
    return pl.pallas_call(
        functools.partial(project_kernel, chunks),
        in_specs=[VMEM, VMEM, VMEM, VMEM, ANY, ANY],
        out_specs=[VMEM, VMEM],
        out_shape=[
            jax.ShapeDtypeStruct((2 * half, steps, q_cols + k_cols), F32),
            jax.ShapeDtypeStruct((n, units), BF16),
        ],
        scratch_shapes=[
            pltpu.VMEM((n, step), F32),
            pltpu.VMEM((n, width), BF16),
            pltpu.VMEM((n, units + k_cols), F32),
            pltpu.SemaphoreType.DMA((chunks,)),
            pltpu.SemaphoreType.DMA((chunks,)),
        ]
        + [pltpu.VMEM((slots, size, step), BF16) for size in sizes],
        compiler_params=params((taken >> 20) + 3),
        cost_estimate=cost(n, w_query, w_keyval, w_gate, w_up),
    )(even, odd, w_query, w_gate, w_up, w_keyval)


def down_kernel(chunks, offset, hidden_ref, w_ref, out_ref, w, out, w_sem, out_sem):
    step = out_ref.shape[1] // chunks

    def cols(c):
        return pl.ds(c * step, step)

    copies = [
        pltpu.make_async_copy(
            w_ref.at[:, pl.ds(offset + c * step, step)], w.at[c], w_sem.at[c]
        )
        for c in range(chunks)
    ]
    out_copies = [
        pltpu.make_async_copy(out.at[c], out_ref.at[:, cols(c)], out_sem.at[c])
        for c in range(chunks)
    ]
    for copy in copies:
        copy.start()
    for c in range(chunks):
        copies[c].wait()
        out[c] = jnp.dot(hidden_ref[...], w[c], preferred_element_type=F32)
        out_copies[c].start()
    for copy in out_copies:
        copy.wait()


def down_part(hidden, w_down, first, last):
    n, units = hidden.shape
    step = w_down.shape[1] // cuts(w_down.shape[1])
    chunks = last - first
    width = chunks * step
    return pl.pallas_call(
        functools.partial(down_kernel, chunks, first * step),
        in_specs=[VMEM, ANY],
        out_specs=ANY,
        out_shape=jax.ShapeDtypeStruct((n, width), F32),
        scratch_shapes=[
            pltpu.VMEM((chunks, units, step), BF16),
            pltpu.VMEM((chunks, n, step), F32),
            pltpu.SemaphoreType.DMA((chunks,)),
            pltpu.SemaphoreType.DMA((chunks,)),
        ],
        compiler_params=params(40),
        cost_estimate=pl.CostEstimate(
            flops=2 * n * units * width, bytes_accessed=2 * units * width, transcendentals=0
        ),
    )(hidden, w_down)


def branch_kernel(
    chunks, attended_ref, first_ref, second_ref, w_ref, keep_ref, send_ref,
    spread, w, part, keep, send, w_sem, part_sem, keep_sem, send_sem,
):
    slots, steps, _ = attended_ref.shape
    half = keep_ref.shape[0]
    step = w_ref.shape[1] // chunks
    middle = first_ref.shape[1] // step
    me = lax.axis_index("gx")

    def cols(c):
        return pl.ds(c * step, step)

    def part_at(c):
        return first_ref.at[:, cols(c)] if c < middle else second_ref.at[:, cols(c - middle)]

    copies = [
        (
            pltpu.make_async_copy(w_ref.at[:, cols(c)], w.at[c], w_sem.at[c]),
            pltpu.make_async_copy(part_at(c), part.at[c], part_sem.at[c]),
        )
        for c in range(chunks)
    ]
    out_copies = [
        (
            pltpu.make_async_copy(keep.at[c], keep_ref.at[:, cols(c)], keep_sem.at[c]),
            pltpu.make_async_copy(send.at[c], send_ref.at[:, cols(c)], send_sem.at[c]),
        )
        for c in range(chunks)
    ]
    for w_copy, part_copy in copies:
        w_copy.start()
        part_copy.start()
    for p in range(slots):
        owner = lax.bitwise_xor(me, slot_at(p, slots // 2))
        spread[p * steps : (p + 1) * steps, :] = attended_ref[owner].astype(F32)
    attended = spread[...].astype(BF16)
    for c in range(chunks):
        for copy in copies[c]:
            copy.wait()
        total = part[c] + jnp.dot(attended, w[c], preferred_element_type=F32)
        keep[c] = total[:half]
        send[c] = total[half:].astype(BF16)
        for copy in out_copies[c]:
            copy.start()
    for pair in out_copies:
        for copy in pair:
            copy.wait()


def branch_parts(attended, first, second, w_out):
    slots, steps, features = attended.shape
    n, width = first.shape[0], w_out.shape[1]
    half = n // 2
    chunks = cuts(width)
    step = width // chunks
    return pl.pallas_call(
        functools.partial(branch_kernel, chunks),
        in_specs=[VMEM, ANY, ANY, ANY],
        out_specs=[ANY, ANY],
        out_shape=[
            jax.ShapeDtypeStruct((half, width), F32),
            jax.ShapeDtypeStruct((half, width), BF16),
        ],
        scratch_shapes=[
            pltpu.VMEM((n, features), F32),
            pltpu.VMEM((chunks, features, step), BF16),
            pltpu.VMEM((chunks, n, step), F32),
            pltpu.VMEM((chunks, half, step), F32),
            pltpu.VMEM((chunks, half, step), BF16),
            pltpu.SemaphoreType.DMA((chunks,)),
            pltpu.SemaphoreType.DMA((chunks,)),
            pltpu.SemaphoreType.DMA((chunks,)),
            pltpu.SemaphoreType.DMA((chunks,)),
        ],
        compiler_params=params(40),
        cost_estimate=cost(n, w_out),
    )(attended, first, second, w_out)


def cut_kernel(keep_ref, came_ref, own_ref, *send_refs):
    steps = own_ref.shape[0]
    total = keep_ref[...] + came_ref[...].astype(F32)
    own_ref[...] = total[:steps]
    for p, send_ref in enumerate(send_refs):
        send_ref[...] = total[(p + 1) * steps : (p + 2) * steps].astype(BF16)


def cut_parts(keep, came, steps):
    half, width = keep.shape
    slots = half // steps
    chunks = 3 if width % 384 == 0 else 1
    step = width // chunks
    whole = pl.BlockSpec((half, step), lambda c: (0, c))
    piece = pl.BlockSpec((steps, step), lambda c: (0, c))
    return pl.pallas_call(
        cut_kernel,
        grid=(chunks,),
        in_specs=[whole, whole],
        out_specs=[piece] * slots,
        out_shape=[jax.ShapeDtypeStruct((steps, width), F32)]
        + [jax.ShapeDtypeStruct((steps, width), BF16)] * (slots - 1),
        compiler_params=params(32),
        cost_estimate=pl.CostEstimate(
            flops=2 * half * width, bytes_accessed=8 * half * width, transcendentals=0
        ),
    )(keep, came)


def rotate(vector, angle_pos):
    half = vector.shape[-1] // 2
    freq = jnp.exp(-math.log(10000.0) * jnp.arange(half, dtype=F32) / half)
    angle = angle_pos[..., None] * freq
    first = vector[..., :half]
    second = vector[..., half:]
    return jnp.concatenate(
        [
            first * jnp.cos(angle) - second * jnp.sin(angle),
            second * jnp.cos(angle) + first * jnp.sin(angle),
        ],
        axis=-1,
    )


def attend(queries, new_keys, new_values, cache_keys, cache_values, lengths):
    steps = queries.shape[1]
    scale = 1.0 / math.sqrt(queries.shape[-1])
    cached = jnp.einsum("rthd,rld->rthl", queries, cache_keys, preferred_element_type=F32) * scale
    live = jnp.arange(cache_keys.shape[1])[None, None, None, :] < lengths[:, None, None, None]
    cached = jnp.where(live, cached, -1e30)
    fresh = jnp.einsum("rthd,red->rthe", queries, new_keys, preferred_element_type=F32) * scale
    known = jnp.arange(steps)[None, :] <= jnp.arange(steps)[:, None]
    fresh = jnp.where(known[None, :, None, :], fresh, -1e30)
    top = jnp.maximum(jnp.max(cached, axis=-1), jnp.max(fresh, axis=-1))
    cached_exp = jnp.exp(cached - top[..., None])
    fresh_exp = jnp.exp(fresh - top[..., None])
    total = jnp.sum(cached_exp, axis=-1) + jnp.sum(fresh_exp, axis=-1)
    cached_w = (cached_exp / total[..., None]).astype(BF16)
    fresh_w = (fresh_exp / total[..., None]).astype(BF16)
    result = jnp.einsum("rthl,rld->rthd", cached_w, cache_values, preferred_element_type=F32)
    result = result + jnp.einsum("rthe,red->rthd", fresh_w, new_values, preferred_element_type=F32)
    return result.astype(BF16)


def swap(value, bits, devices):
    return lax.ppermute(value, "gx", [(i, i ^ bits) for i in range(devices)])


def gather_rows(piece, devices):
    outer = min(4, devices // 2)
    inner = devices // (2 * outer)
    near = [piece] + [swap(piece, 2 * inner * a, devices) for a in range(1, outer)]
    far = [near] + [[swap(p, 2 * b, devices) for p in near] for b in range(1, inner)]
    even = jnp.stack([far[b][a] for a in range(outer) for b in range(inner)])
    return even, swap(even, 1, devices)


def local(
    tokens,
    norm_gain,
    w_query,
    w_keyval,
    w_gate,
    w_up,
    w_out,
    w_down,
    cache_keys,
    cache_values,
    lengths,
    positions,
):
    steps, rows, width = tokens.shape
    head = cache_keys.shape[2]
    query_cols = w_query.shape[0]
    devices = lax.axis_size("gx")
    batch = steps * rows
    own_tokens = tokens.reshape(batch, width)
    even, odd = gather_rows(layer_norm(own_tokens, norm_gain), devices)
    projected, hidden = project(even, odd, w_query, w_keyval, w_gate, w_up)

    chunks = cuts(width)
    first = down_part(hidden, w_down, 0, chunks // 2)
    arrived = lax.all_to_all(projected, "gx", split_axis=0, concat_axis=0, tiled=True)
    arrived, first = lax.optimization_barrier((arrived, first))
    arrived = arrived.reshape(devices, steps, rows, -1).transpose(2, 1, 0, 3)
    query = arrived[..., :query_cols].reshape(rows, steps, -1, head)
    keyval = arrived[..., query_cols:].reshape(rows, steps, 2 * head)
    angle_pos = (positions[:, None] + jnp.arange(steps)[None, :]).astype(F32)
    rotated = rotate(query, angle_pos[:, :, None]).astype(BF16)
    new_keys = rotate(keyval[..., :head], angle_pos).astype(BF16)
    new_values = keyval[..., head:].astype(BF16)
    attended = attend(rotated, new_keys, new_values, cache_keys, cache_values, lengths)
    attended = attended.reshape(rows, steps, devices, -1).transpose(2, 1, 0, 3)
    attended = attended.reshape(devices, batch, -1)
    attended, hidden = lax.optimization_barrier((attended, hidden))
    attended = lax.all_to_all(attended, "gx", split_axis=0, concat_axis=0, tiled=True)

    second = down_part(hidden, w_down, chunks // 2, chunks)
    keep, send = branch_parts(attended, first, second, w_out)
    pieces = cut_parts(keep, swap(send, 1, devices), batch)
    branch = pieces[0]
    for place in range(1, devices // 2):
        branch = branch + swap(pieces[place], 2 * place, devices).astype(F32)
    result = (own_tokens.astype(F32) + branch).astype(BF16)
    return result.reshape(tokens.shape)


def solution(mesh):
    in_specs = (
        P(None, ("groups", "gx"), None),
        P(),
        P("gx", None),
        P("gx", None),
        P("gx", None),
        P("gx", None),
        P("gx", None),
        P("gx", None),
        P(("groups", "gx"), None, None),
        P(("groups", "gx"), None, None),
        P(("groups", "gx")),
        P(("groups", "gx")),
    )
    out_specs = P(None, ("groups", "gx"), None)
    return jax.shard_map(local, mesh=mesh, in_specs=in_specs, out_specs=out_specs, check_vma=False)
```

```python
import functools
import math

import jax
import jax.numpy as jnp
from jax import lax
from jax.experimental import pallas as pl
from jax.experimental.pallas import tpu as pltpu
from jax.sharding import PartitionSpec as P

F32 = jnp.float32
BF16 = jnp.bfloat16
NT = (((1,), (1,)), ((), ()))
ANY = pl.BlockSpec(memory_space=pl.ANY)
VMEM = pl.BlockSpec(memory_space=pltpu.VMEM)


def params(mib):
    return pltpu.CompilerParams(vmem_limit_bytes=mib << 20)


def cost(rows, *weights):
    size = sum(math.prod(w.shape) for w in weights)
    return pl.CostEstimate(flops=2 * rows * size, bytes_accessed=2 * size, transcendentals=0)


def slot_at(place, half):
    return 2 * place if place < half else 2 * (place - half) + 1


def cuts(width):
    for count in (8, 9, 6, 4, 3, 2):
        if width % (128 * count) == 0:
            return count
    return 1


def center_kernel(tokens_ref, out_ref):
    values = tokens_ref[...].astype(F32)
    centered = values - jnp.mean(values, axis=-1, keepdims=True)
    spread = jnp.mean(centered * centered, axis=-1, keepdims=True)
    out_ref[...] = centered / jnp.sqrt(spread + 1e-05)


def gain_kernel(values_ref, gain_ref, out_ref):
    out_ref[...] = (values_ref[...] * gain_ref[...]).astype(BF16)


def layer_norm(tokens, norm_gain):
    centered = pl.pallas_call(
        center_kernel,
        out_shape=jax.ShapeDtypeStruct(tokens.shape, F32),
        compiler_params=params(4),
        cost_estimate=pl.CostEstimate(
            flops=25 * 10**9, bytes_accessed=75 * 10**6, transcendentals=0
        ),
    )(tokens)
    return pl.pallas_call(
        gain_kernel,
        out_shape=jax.ShapeDtypeStruct(tokens.shape, BF16),
        compiler_params=params(4),
    )(centered, norm_gain.reshape(1, -1))


def project_kernel(
    chunks, even_ref, odd_ref, wq_ref, wg_ref, wu_ref, wk_ref, out_ref, hidden_ref,
    rows, acc, sem_u, sem_k, *streams,
):
    half, steps, width = even_ref.shape
    step = width // chunks
    units = wu_ref.shape[0]
    q_cols = wq_ref.shape[0]

    def cols(c):
        return pl.ds(c * step, step)

    slots = streams[0].shape[0]

    def keyval_place(c):
        if len(streams) == 2:
            return streams[1].at[c % slots]
        return streams[0].at[c % slots, pl.ds(units, wk_ref.shape[0])]

    def up_place(c):
        if len(streams) == 2:
            return streams[0].at[c % slots]
        return streams[0].at[c % slots, pl.ds(0, units)]

    copies = [
        (
            pltpu.make_async_copy(wu_ref.at[:, cols(c)], up_place(c), sem_u.at[c]),
            pltpu.make_async_copy(wk_ref.at[:, cols(c)], keyval_place(c), sem_k.at[c]),
        )
        for c in range(chunks)
    ]
    for pair in copies[:slots]:
        for copy in pair:
            copy.start()
    acc[...] = jnp.zeros_like(acc)
    query = jnp.zeros((rows.shape[0], q_cols), F32)
    gate = jnp.zeros((rows.shape[0], units), F32)
    for c in range(chunks):
        part = slice(c * step, (c + 1) * step)
        for p in range(half):
            rows[p * steps : (p + 1) * steps, part] = even_ref[p, :, part]
            q = half + p
            rows[q * steps : (q + 1) * steps, part] = odd_ref[p, :, part]
        block = rows[:, part]
        query += lax.dot_general(block, wq_ref[:, part], NT, preferred_element_type=F32)
        gate += lax.dot_general(block, wg_ref[:, part], NT, preferred_element_type=F32)
    for c in range(chunks):
        for copy in copies[c]:
            copy.wait()
        first = 0
        for stream in streams:
            last = first + stream.shape[1]
            acc[:, first:last] += lax.dot_general(
                rows[:, c * step : (c + 1) * step], stream[c % slots], NT, preferred_element_type=F32
            )
            first = last
        if c + slots < chunks:
            for copy in copies[c + slots]:
                copy.start()
    me = lax.axis_index("gx")
    for p in range(2 * half):
        owner = lax.bitwise_xor(me, slot_at(p, half))
        out_ref[owner, :, :q_cols] = query[p * steps : (p + 1) * steps]
        out_ref[owner, :, q_cols:] = acc[p * steps : (p + 1) * steps, units:]
    hidden_ref[...] = (jax.nn.silu(gate) * acc[:, :units]).astype(BF16)


def project(even, odd, w_query, w_keyval, w_gate, w_up):
    half, steps, width = even.shape
    n = 2 * half * steps
    chunks = cuts(width)
    step = width // chunks
    q_cols, k_cols, units = w_query.shape[0], w_keyval.shape[0], w_up.shape[0]
    together = k_cols % 16 == 0 and units % 16 == 0
    sizes = [units + k_cols] if together else [units, k_cols]
    slots = min(chunks, 4)
    taken = 2 * slots * step * (units + k_cols) + 6 * n * width + 4 * n * (step + 4 * units)
    near = 2 * width * (q_cols + units)
    taken += near if near < 8 << 20 else 0
    return pl.pallas_call(
        functools.partial(project_kernel, chunks),
        in_specs=[VMEM, VMEM, VMEM, VMEM, ANY, ANY],
        out_specs=[VMEM, VMEM],
        out_shape=[
            jax.ShapeDtypeStruct((2 * half, steps, q_cols + k_cols), F32),
            jax.ShapeDtypeStruct((n, units), BF16),
        ],
        scratch_shapes=[
            pltpu.VMEM((n, width), BF16),
            pltpu.VMEM((n, units + k_cols), F32),
            pltpu.SemaphoreType.DMA((chunks,)),
            pltpu.SemaphoreType.DMA((chunks,)),
        ]
        + [pltpu.VMEM((slots, size, step), BF16) for size in sizes],
        compiler_params=params((taken >> 20) + 3),
        cost_estimate=cost(n, w_query, w_keyval, w_gate, w_up),
    )(even, odd, w_query, w_gate, w_up, w_keyval)


def down_kernel(chunks, offset, hidden_ref, w_ref, out_ref, w, out, w_sem, out_sem):
    step = out_ref.shape[1] // chunks

    def cols(c):
        return pl.ds(c * step, step)

    copies = [
        pltpu.make_async_copy(
            w_ref.at[:, pl.ds(offset + c * step, step)], w.at[c], w_sem.at[c]
        )
        for c in range(chunks)
    ]
    out_copies = [
        pltpu.make_async_copy(out.at[c], out_ref.at[:, cols(c)], out_sem.at[c])
        for c in range(chunks)
    ]
    for copy in copies:
        copy.start()
    for c in range(chunks):
        copies[c].wait()
        out[c] = jnp.dot(hidden_ref[...], w[c], preferred_element_type=F32)
        out_copies[c].start()
    for copy in out_copies:
        copy.wait()


def down_part(hidden, w_down, first, last):
    n, units = hidden.shape
    step = w_down.shape[1] // cuts(w_down.shape[1])
    chunks = last - first
    width = chunks * step
    return pl.pallas_call(
        functools.partial(down_kernel, chunks, first * step),
        in_specs=[VMEM, ANY],
        out_specs=ANY,
        out_shape=jax.ShapeDtypeStruct((n, width), F32),
        scratch_shapes=[
            pltpu.VMEM((chunks, units, step), BF16),
            pltpu.VMEM((chunks, n, step), F32),
            pltpu.SemaphoreType.DMA((chunks,)),
            pltpu.SemaphoreType.DMA((chunks,)),
        ],
        compiler_params=params(40),
        cost_estimate=pl.CostEstimate(
            flops=2 * n * units * width, bytes_accessed=2 * units * width, transcendentals=0
        ),
    )(hidden, w_down)


def branch_kernel(
    chunks, attended_ref, first_ref, second_ref, w_ref, keep_ref, send_ref,
    spread, w, part, keep, send, w_sem, part_sem, keep_sem, send_sem,
):
    slots, steps, _ = attended_ref.shape
    half = keep_ref.shape[0]
    step = w_ref.shape[1] // chunks
    middle = first_ref.shape[1] // step
    me = lax.axis_index("gx")

    def cols(c):
        return pl.ds(c * step, step)

    def part_at(c):
        return first_ref.at[:, cols(c)] if c < middle else second_ref.at[:, cols(c - middle)]

    copies = [
        (
            pltpu.make_async_copy(w_ref.at[:, cols(c)], w.at[c], w_sem.at[c]),
            pltpu.make_async_copy(part_at(c), part.at[c], part_sem.at[c]),
        )
        for c in range(chunks)
    ]
    out_copies = [
        (
            pltpu.make_async_copy(keep.at[c], keep_ref.at[:, cols(c)], keep_sem.at[c]),
            pltpu.make_async_copy(send.at[c], send_ref.at[:, cols(c)], send_sem.at[c]),
        )
        for c in range(chunks)
    ]
    for w_copy, part_copy in copies:
        w_copy.start()
        part_copy.start()
    for p in range(slots):
        owner = lax.bitwise_xor(me, slot_at(p, slots // 2))
        spread[p * steps : (p + 1) * steps, :] = attended_ref[owner].astype(F32)
    attended = spread[...].astype(BF16)
    for c in range(chunks):
        for copy in copies[c]:
            copy.wait()
        total = part[c] + jnp.dot(attended, w[c], preferred_element_type=F32)
        keep[c] = total[:half]
        send[c] = total[half:].astype(BF16)
        for copy in out_copies[c]:
            copy.start()
    for pair in out_copies:
        for copy in pair:
            copy.wait()


def branch_parts(attended, first, second, w_out):
    slots, steps, features = attended.shape
    n, width = first.shape[0], w_out.shape[1]
    half = n // 2
    chunks = cuts(width)
    step = width // chunks
    return pl.pallas_call(
        functools.partial(branch_kernel, chunks),
        in_specs=[VMEM, ANY, ANY, ANY],
        out_specs=[ANY, ANY],
        out_shape=[
            jax.ShapeDtypeStruct((half, width), F32),
            jax.ShapeDtypeStruct((half, width), BF16),
        ],
        scratch_shapes=[
            pltpu.VMEM((n, features), F32),
            pltpu.VMEM((chunks, features, step), BF16),
            pltpu.VMEM((chunks, n, step), F32),
            pltpu.VMEM((chunks, half, step), F32),
            pltpu.VMEM((chunks, half, step), BF16),
            pltpu.SemaphoreType.DMA((chunks,)),
            pltpu.SemaphoreType.DMA((chunks,)),
            pltpu.SemaphoreType.DMA((chunks,)),
            pltpu.SemaphoreType.DMA((chunks,)),
        ],
        compiler_params=params(40),
        cost_estimate=cost(n, w_out),
    )(attended, first, second, w_out)


def cut_kernel(keep_ref, came_ref, own_ref, *send_refs):
    steps = own_ref.shape[0]
    total = keep_ref[...] + came_ref[...].astype(F32)
    own_ref[...] = total[:steps]
    for p, send_ref in enumerate(send_refs):
        send_ref[...] = total[(p + 1) * steps : (p + 2) * steps].astype(BF16)


def cut_parts(keep, came, steps):
    half, width = keep.shape
    slots = half // steps
    chunks = 3 if width % 384 == 0 else 1
    step = width // chunks
    whole = pl.BlockSpec((half, step), lambda c: (0, c))
    piece = pl.BlockSpec((steps, step), lambda c: (0, c))
    return pl.pallas_call(
        cut_kernel,
        grid=(chunks,),
        in_specs=[whole, whole],
        out_specs=[piece] * slots,
        out_shape=[jax.ShapeDtypeStruct((steps, width), F32)]
        + [jax.ShapeDtypeStruct((steps, width), BF16)] * (slots - 1),
        compiler_params=params(32),
        cost_estimate=pl.CostEstimate(
            flops=2 * half * width, bytes_accessed=8 * half * width, transcendentals=0
        ),
    )(keep, came)


def rotate(vector, angle_pos):
    half = vector.shape[-1] // 2
    freq = jnp.exp(-math.log(10000.0) * jnp.arange(half, dtype=F32) / half)
    angle = angle_pos[..., None] * freq
    first = vector[..., :half]
    second = vector[..., half:]
    return jnp.concatenate(
        [
            first * jnp.cos(angle) - second * jnp.sin(angle),
            second * jnp.cos(angle) + first * jnp.sin(angle),
        ],
        axis=-1,
    )


def attend(queries, new_keys, new_values, cache_keys, cache_values, lengths):
    steps = queries.shape[1]
    scale = 1.0 / math.sqrt(queries.shape[-1])
    cached = jnp.einsum("rthd,rld->rthl", queries, cache_keys, preferred_element_type=F32) * scale
    live = jnp.arange(cache_keys.shape[1])[None, None, None, :] < lengths[:, None, None, None]
    cached = jnp.where(live, cached, -1e30)
    fresh = jnp.einsum("rthd,red->rthe", queries, new_keys, preferred_element_type=F32) * scale
    known = jnp.arange(steps)[None, :] <= jnp.arange(steps)[:, None]
    fresh = jnp.where(known[None, :, None, :], fresh, -1e30)
    top = jnp.maximum(jnp.max(cached, axis=-1), jnp.max(fresh, axis=-1))
    cached_exp = jnp.exp(cached - top[..., None])
    fresh_exp = jnp.exp(fresh - top[..., None])
    total = jnp.sum(cached_exp, axis=-1) + jnp.sum(fresh_exp, axis=-1)
    cached_w = (cached_exp / total[..., None]).astype(BF16)
    fresh_w = (fresh_exp / total[..., None]).astype(BF16)
    result = jnp.einsum("rthl,rld->rthd", cached_w, cache_values, preferred_element_type=F32)
    result = result + jnp.einsum("rthe,red->rthd", fresh_w, new_values, preferred_element_type=F32)
    return result.astype(BF16)


def swap(value, bits, devices):
    return lax.ppermute(value, "gx", [(i, i ^ bits) for i in range(devices)])


def gather_rows(piece, devices):
    outer = min(4, devices // 2)
    inner = devices // (2 * outer)
    near = [piece] + [swap(piece, 2 * inner * a, devices) for a in range(1, outer)]
    far = [near] + [[swap(p, 2 * b, devices) for p in near] for b in range(1, inner)]
    even = jnp.stack([far[b][a] for a in range(outer) for b in range(inner)])
    return even, swap(even, 1, devices)


def local(
    tokens,
    norm_gain,
    w_query,
    w_keyval,
    w_gate,
    w_up,
    w_out,
    w_down,
    cache_keys,
    cache_values,
    lengths,
    positions,
):
    steps, rows, width = tokens.shape
    head = cache_keys.shape[2]
    query_cols = w_query.shape[0]
    devices = lax.axis_size("gx")
    batch = steps * rows
    own_tokens = tokens.reshape(batch, width)
    even, odd = gather_rows(layer_norm(own_tokens, norm_gain), devices)
    projected, hidden = project(even, odd, w_query, w_keyval, w_gate, w_up)

    chunks = cuts(width)
    first = down_part(hidden, w_down, 0, chunks // 2)
    arrived = lax.all_to_all(projected, "gx", split_axis=0, concat_axis=0, tiled=True)
    arrived, first = lax.optimization_barrier((arrived, first))
    arrived = arrived.reshape(devices, steps, rows, -1).transpose(2, 1, 0, 3)
    query = arrived[..., :query_cols].reshape(rows, steps, -1, head)
    keyval = arrived[..., query_cols:].reshape(rows, steps, 2 * head)
    angle_pos = (positions[:, None] + jnp.arange(steps)[None, :]).astype(F32)
    rotated = rotate(query, angle_pos[:, :, None]).astype(BF16)
    new_keys = rotate(keyval[..., :head], angle_pos).astype(BF16)
    new_values = keyval[..., head:].astype(BF16)
    attended = attend(rotated, new_keys, new_values, cache_keys, cache_values, lengths)
    attended = attended.reshape(rows, steps, devices, -1).transpose(2, 1, 0, 3)
    attended = attended.reshape(devices, batch, -1)
    attended, hidden = lax.optimization_barrier((attended, hidden))
    attended = lax.all_to_all(attended, "gx", split_axis=0, concat_axis=0, tiled=True)

    second = down_part(hidden, w_down, chunks // 2, chunks)
    keep, send = branch_parts(attended, first, second, w_out)
    pieces = cut_parts(keep, swap(send, 1, devices), batch)
    branch = pieces[0]
    for place in reversed(range(1, devices // 2)):
        branch = branch + swap(pieces[place], 2 * place, devices).astype(F32)
    result = (own_tokens.astype(F32) + branch).astype(BF16)
    return result.reshape(tokens.shape)


def solution(mesh):
    in_specs = (
        P(None, ("groups", "gx"), None),
        P(),
        P("gx", None),
        P("gx", None),
        P("gx", None),
        P("gx", None),
        P("gx", None),
        P("gx", None),
        P(("groups", "gx"), None, None),
        P(("groups", "gx"), None, None),
        P(("groups", "gx")),
        P(("groups", "gx")),
    )
    out_specs = P(None, ("groups", "gx"), None)
    return jax.shard_map(local, mesh=mesh, in_specs=in_specs, out_specs=out_specs, check_vma=False)
```

```python
import functools
import math

import jax
import jax.numpy as jnp
from jax import lax
from jax.experimental import pallas as pl
from jax.experimental.pallas import tpu as pltpu
from jax.sharding import PartitionSpec as P

F32 = jnp.float32
BF16 = jnp.bfloat16
NT = (((1,), (1,)), ((), ()))
ANY = pl.BlockSpec(memory_space=pl.ANY)
VMEM = pl.BlockSpec(memory_space=pltpu.VMEM)


def params(mib):
    return pltpu.CompilerParams(vmem_limit_bytes=mib << 20)


def cost(rows, *weights):
    size = sum(math.prod(w.shape) for w in weights)
    return pl.CostEstimate(flops=2 * rows * size, bytes_accessed=2 * size, transcendentals=0)


def slot_at(place, half):
    return 2 * place if place < half else 2 * (place - half) + 1


def cuts(width):
    for count in (8, 9, 6, 4, 3, 2):
        if width % (128 * count) == 0:
            return count
    return 1


def center_kernel(tokens_ref, out_ref):
    values = tokens_ref[...].astype(F32)
    centered = values - jnp.mean(values, axis=-1, keepdims=True)
    spread = jnp.mean(centered * centered, axis=-1, keepdims=True)
    out_ref[...] = centered / jnp.sqrt(spread + 1e-05)


def gain_kernel(values_ref, gain_ref, out_ref):
    out_ref[...] = (values_ref[...] * gain_ref[...]).astype(BF16)


def layer_norm(tokens, norm_gain):
    centered = pl.pallas_call(
        center_kernel,
        out_shape=jax.ShapeDtypeStruct(tokens.shape, F32),
        compiler_params=params(4),
        cost_estimate=pl.CostEstimate(
            flops=25 * 10**9, bytes_accessed=75 * 10**6, transcendentals=0
        ),
    )(tokens)
    return pl.pallas_call(
        gain_kernel,
        out_shape=jax.ShapeDtypeStruct(tokens.shape, BF16),
        compiler_params=params(4),
    )(centered, norm_gain.reshape(1, -1))


def project_kernel(
    chunks, even_ref, odd_ref, wq_ref, wg_ref, wu_ref, wk_ref, out_ref, hidden_ref,
    rows, acc, sem_u, sem_k, *streams,
):
    half, steps, width = even_ref.shape
    step = width // chunks
    units = wu_ref.shape[0]
    q_cols = wq_ref.shape[0]

    def cols(c):
        return pl.ds(c * step, step)

    slots = streams[0].shape[0]

    def keyval_place(c):
        if len(streams) == 2:
            return streams[1].at[c % slots]
        return streams[0].at[c % slots, pl.ds(units, wk_ref.shape[0])]

    def up_place(c):
        if len(streams) == 2:
            return streams[0].at[c % slots]
        return streams[0].at[c % slots, pl.ds(0, units)]

    copies = [
        (
            pltpu.make_async_copy(wu_ref.at[:, cols(c)], up_place(c), sem_u.at[c]),
            pltpu.make_async_copy(wk_ref.at[:, cols(c)], keyval_place(c), sem_k.at[c]),
        )
        for c in range(chunks)
    ]
    for pair in copies[:slots]:
        for copy in pair:
            copy.start()
    acc[...] = jnp.zeros_like(acc)
    query = jnp.zeros((rows.shape[0], q_cols), F32)
    gate = jnp.zeros((rows.shape[0], units), F32)
    for c in range(chunks):
        part = slice(c * step, (c + 1) * step)
        for p in range(half):
            rows[p * steps : (p + 1) * steps, part] = even_ref[p, :, part]
            q = half + p
            rows[q * steps : (q + 1) * steps, part] = odd_ref[p, :, part]
        block = rows[:, part]
        query += lax.dot_general(block, wq_ref[:, part], NT, preferred_element_type=F32)
        gate += lax.dot_general(block, wg_ref[:, part], NT, preferred_element_type=F32)
    for c in range(chunks):
        for copy in copies[c]:
            copy.wait()
        first = 0
        for stream in streams:
            last = first + stream.shape[1]
            acc[:, first:last] += lax.dot_general(
                rows[:, c * step : (c + 1) * step], stream[c % slots], NT, preferred_element_type=F32
            )
            first = last
        if c + slots < chunks:
            for copy in copies[c + slots]:
                copy.start()
    me = lax.axis_index("gx")
    for p in range(2 * half):
        owner = lax.bitwise_xor(me, slot_at(p, half))
        out_ref[owner, :, :q_cols] = query[p * steps : (p + 1) * steps]
        out_ref[owner, :, q_cols:] = acc[p * steps : (p + 1) * steps, units:]
    hidden_ref[...] = (jax.nn.silu(gate) * acc[:, :units]).astype(BF16)


def project(even, odd, w_query, w_keyval, w_gate, w_up):
    half, steps, width = even.shape
    n = 2 * half * steps
    chunks = cuts(width)
    step = width // chunks
    q_cols, k_cols, units = w_query.shape[0], w_keyval.shape[0], w_up.shape[0]
    together = k_cols % 16 == 0 and units % 16 == 0
    sizes = [units + k_cols] if together else [units, k_cols]
    slots = min(chunks, 4)
    taken = 2 * slots * step * (units + k_cols) + 6 * n * width + 4 * n * (step + 4 * units)
    near = 2 * width * (q_cols + units)
    taken += near if near < 8 << 20 else 0
    return pl.pallas_call(
        functools.partial(project_kernel, chunks),
        in_specs=[VMEM, VMEM, VMEM, VMEM, ANY, ANY],
        out_specs=[VMEM, VMEM],
        out_shape=[
            jax.ShapeDtypeStruct((2 * half, steps, q_cols + k_cols), F32),
            jax.ShapeDtypeStruct((n, units), BF16),
        ],
        scratch_shapes=[
            pltpu.VMEM((n, width), BF16),
            pltpu.VMEM((n, units + k_cols), F32),
            pltpu.SemaphoreType.DMA((chunks,)),
            pltpu.SemaphoreType.DMA((chunks,)),
        ]
        + [pltpu.VMEM((slots, size, step), BF16) for size in sizes],
        compiler_params=params((taken >> 20) + 3),
        cost_estimate=cost(n, w_query, w_keyval, w_gate, w_up),
    )(even, odd, w_query, w_gate, w_up, w_keyval)


def down_kernel(chunks, offset, hidden_ref, w_ref, out_ref, w, out, w_sem, out_sem):
    step = out_ref.shape[1] // chunks

    def cols(c):
        return pl.ds(c * step, step)

    copies = [
        pltpu.make_async_copy(
            w_ref.at[:, pl.ds(offset + c * step, step)], w.at[c], w_sem.at[c]
        )
        for c in range(chunks)
    ]
    out_copies = [
        pltpu.make_async_copy(out.at[c], out_ref.at[:, cols(c)], out_sem.at[c])
        for c in range(chunks)
    ]
    for copy in copies:
        copy.start()
    for c in range(chunks):
        copies[c].wait()
        out[c] = jnp.dot(hidden_ref[...], w[c], preferred_element_type=F32)
        out_copies[c].start()
    for copy in out_copies:
        copy.wait()


def down_part(hidden, w_down, first, last):
    n, units = hidden.shape
    step = w_down.shape[1] // cuts(w_down.shape[1])
    chunks = last - first
    width = chunks * step
    return pl.pallas_call(
        functools.partial(down_kernel, chunks, first * step),
        in_specs=[VMEM, ANY],
        out_specs=ANY,
        out_shape=jax.ShapeDtypeStruct((n, width), F32),
        scratch_shapes=[
            pltpu.VMEM((chunks, units, step), BF16),
            pltpu.VMEM((chunks, n, step), F32),
            pltpu.SemaphoreType.DMA((chunks,)),
            pltpu.SemaphoreType.DMA((chunks,)),
        ],
        compiler_params=params(40),
        cost_estimate=pl.CostEstimate(
            flops=2 * n * units * width, bytes_accessed=2 * units * width, transcendentals=0
        ),
    )(hidden, w_down)


def branch_kernel(
    chunks, attended_ref, first_ref, second_ref, w_ref, keep_ref, send_ref,
    spread, w, part, keep, send, w_sem, part_sem, keep_sem, send_sem,
):
    slots, steps, _ = attended_ref.shape
    half = keep_ref.shape[0]
    step = w_ref.shape[1] // chunks
    middle = first_ref.shape[1] // step
    me = lax.axis_index("gx")

    def cols(c):
        return pl.ds(c * step, step)

    def part_at(c):
        return first_ref.at[:, cols(c)] if c < middle else second_ref.at[:, cols(c - middle)]

    copies = [
        (
            pltpu.make_async_copy(w_ref.at[:, cols(c)], w.at[c], w_sem.at[c]),
            pltpu.make_async_copy(part_at(c), part.at[c], part_sem.at[c]),
        )
        for c in range(chunks)
    ]
    out_copies = [
        (
            pltpu.make_async_copy(keep.at[c], keep_ref.at[:, cols(c)], keep_sem.at[c]),
            pltpu.make_async_copy(send.at[c], send_ref.at[:, cols(c)], send_sem.at[c]),
        )
        for c in range(chunks)
    ]
    for w_copy, part_copy in copies:
        w_copy.start()
        part_copy.start()
    for p in range(slots):
        owner = lax.bitwise_xor(me, slot_at(p, slots // 2))
        spread[p * steps : (p + 1) * steps, :] = attended_ref[owner].astype(F32)
    attended = spread[...].astype(BF16)
    for c in range(chunks):
        for copy in copies[c]:
            copy.wait()
        total = part[c] + jnp.dot(attended, w[c], preferred_element_type=F32)
        keep[c] = total[:half]
        send[c] = total[half:].astype(BF16)
        for copy in out_copies[c]:
            copy.start()
    for pair in out_copies:
        for copy in pair:
            copy.wait()


def branch_parts(attended, first, second, w_out):
    slots, steps, features = attended.shape
    n, width = first.shape[0], w_out.shape[1]
    half = n // 2
    chunks = cuts(width)
    step = width // chunks
    return pl.pallas_call(
        functools.partial(branch_kernel, chunks),
        in_specs=[VMEM, ANY, ANY, ANY],
        out_specs=[ANY, ANY],
        out_shape=[
            jax.ShapeDtypeStruct((half, width), F32),
            jax.ShapeDtypeStruct((half, width), BF16),
        ],
        scratch_shapes=[
            pltpu.VMEM((n, features), F32),
            pltpu.VMEM((chunks, features, step), BF16),
            pltpu.VMEM((chunks, n, step), F32),
            pltpu.VMEM((chunks, half, step), F32),
            pltpu.VMEM((chunks, half, step), BF16),
            pltpu.SemaphoreType.DMA((chunks,)),
            pltpu.SemaphoreType.DMA((chunks,)),
            pltpu.SemaphoreType.DMA((chunks,)),
            pltpu.SemaphoreType.DMA((chunks,)),
        ],
        compiler_params=params(40),
        cost_estimate=cost(n, w_out),
    )(attended, first, second, w_out)


def cut_kernel(plan, keep_ref, came_ref, own_ref, far_ref, *send_refs):
    near, kept, sent = plan
    steps = own_ref.shape[0]
    total = keep_ref[...] + came_ref[...].astype(F32)

    def piece(place):
        return total[place * steps : (place + 1) * steps]

    own_ref[...] = piece(0)
    for k, place in enumerate(kept):
        far_ref[k] = piece(place)
    for place, send_ref in zip(near, send_refs):
        send_ref[...] = piece(place).astype(BF16)
    for group, send_ref in zip(sent, send_refs[len(near) :]):
        for k, place in enumerate(group):
            send_ref[k] = piece(place).astype(BF16)


def cut_parts(keep, came, steps, plan):
    half, width = keep.shape
    near, kept, sent = plan
    chunks = 3 if width % 384 == 0 else 1
    step = width // chunks
    whole = pl.BlockSpec((half, step), lambda c: (0, c))
    piece = pl.BlockSpec((steps, step), lambda c: (0, c))
    pair = pl.BlockSpec((len(kept), steps, step), lambda c: (0, 0, c))
    pair_shape = (len(kept), steps, width)
    return pl.pallas_call(
        functools.partial(cut_kernel, plan),
        grid=(chunks,),
        in_specs=[whole, whole],
        out_specs=[piece, pair] + [piece] * len(near) + [pair] * len(sent),
        out_shape=[
            jax.ShapeDtypeStruct((steps, width), F32),
            jax.ShapeDtypeStruct(pair_shape, F32),
        ]
        + [jax.ShapeDtypeStruct((steps, width), BF16)] * len(near)
        + [jax.ShapeDtypeStruct(pair_shape, BF16)] * len(sent),
        compiler_params=params(32),
        cost_estimate=pl.CostEstimate(
            flops=2 * half * width, bytes_accessed=8 * half * width, transcendentals=0
        ),
    )(keep, came)


def far_kernel(far_ref, *refs):
    count = far_ref.shape[0]
    for k in range(count):
        total = far_ref[k]
        for came_ref in refs[:-count]:
            total = total + came_ref[k].astype(F32)
        refs[len(refs) - count + k][...] = total.astype(BF16)


def far_parts(far, arrived):
    count, steps, width = far.shape
    chunks = 3 if width % 384 == 0 else 1
    step = width // chunks
    pair = pl.BlockSpec((count, steps, step), lambda c: (0, 0, c))
    piece = pl.BlockSpec((steps, step), lambda c: (0, c))
    return pl.pallas_call(
        far_kernel,
        grid=(chunks,),
        in_specs=[pair] * (1 + len(arrived)),
        out_specs=[piece] * count,
        out_shape=[jax.ShapeDtypeStruct((steps, width), BF16)] * count,
        compiler_params=params(32),
        cost_estimate=pl.CostEstimate(
            flops=far.size, bytes_accessed=8 * far.size, transcendentals=0
        ),
    )(far, *arrived)


def rotate(vector, angle_pos):
    half = vector.shape[-1] // 2
    freq = jnp.exp(-math.log(10000.0) * jnp.arange(half, dtype=F32) / half)
    angle = angle_pos[..., None] * freq
    first = vector[..., :half]
    second = vector[..., half:]
    return jnp.concatenate(
        [
            first * jnp.cos(angle) - second * jnp.sin(angle),
            second * jnp.cos(angle) + first * jnp.sin(angle),
        ],
        axis=-1,
    )


def attend(queries, new_keys, new_values, cache_keys, cache_values, lengths):
    steps = queries.shape[1]
    scale = 1.0 / math.sqrt(queries.shape[-1])
    cached = jnp.einsum("rthd,rld->rthl", queries, cache_keys, preferred_element_type=F32) * scale
    live = jnp.arange(cache_keys.shape[1])[None, None, None, :] < lengths[:, None, None, None]
    cached = jnp.where(live, cached, -1e30)
    fresh = jnp.einsum("rthd,red->rthe", queries, new_keys, preferred_element_type=F32) * scale
    known = jnp.arange(steps)[None, :] <= jnp.arange(steps)[:, None]
    fresh = jnp.where(known[None, :, None, :], fresh, -1e30)
    top = jnp.maximum(jnp.max(cached, axis=-1), jnp.max(fresh, axis=-1))
    cached_exp = jnp.exp(cached - top[..., None])
    fresh_exp = jnp.exp(fresh - top[..., None])
    total = jnp.sum(cached_exp, axis=-1) + jnp.sum(fresh_exp, axis=-1)
    cached_w = (cached_exp / total[..., None]).astype(BF16)
    fresh_w = (fresh_exp / total[..., None]).astype(BF16)
    result = jnp.einsum("rthl,rld->rthd", cached_w, cache_values, preferred_element_type=F32)
    result = result + jnp.einsum("rthe,red->rthd", fresh_w, new_values, preferred_element_type=F32)
    return result.astype(BF16)


def swap(value, bits, devices):
    return lax.ppermute(value, "gx", [(i, i ^ bits) for i in range(devices)])


def gather_rows(piece, devices):
    outer = min(4, devices // 2)
    inner = devices // (2 * outer)
    near = [piece] + [swap(piece, 2 * inner * a, devices) for a in range(1, outer)]
    far = [near] + [[swap(p, 2 * b, devices) for p in near] for b in range(1, inner)]
    even = jnp.stack([far[b][a] for a in range(outer) for b in range(inner)])
    return even, swap(even, 1, devices)


def scatter_sums(keep, came, batch, devices):
    outer = min(4, devices // 2)
    inner = devices // (2 * outer)
    middle = outer // 2
    near = [p for p in range(1, middle * inner)]
    kept = [a * inner for a in range(middle, outer)]
    sent = [[p + b for p in kept] for b in range(1, inner)]
    own, far, *sends = cut_parts(keep, came, batch, (near, kept, sent))
    arrived = [
        swap(group, 2 * b, devices) for b, group in zip(range(1, inner), sends[len(near) :])
    ]
    parts = [swap(piece, 2 * p, devices) for p, piece in zip(near, sends)]
    late = [swap(piece, 2 * p, devices) for p, piece in zip(kept, far_parts(far, arrived))]
    for part in parts + late:
        own = own + part.astype(F32)
    return own


def local(
    tokens,
    norm_gain,
    w_query,
    w_keyval,
    w_gate,
    w_up,
    w_out,
    w_down,
    cache_keys,
    cache_values,
    lengths,
    positions,
):
    steps, rows, width = tokens.shape
    head = cache_keys.shape[2]
    query_cols = w_query.shape[0]
    devices = lax.axis_size("gx")
    batch = steps * rows
    own_tokens = tokens.reshape(batch, width)
    even, odd = gather_rows(layer_norm(own_tokens, norm_gain), devices)
    projected, hidden = project(even, odd, w_query, w_keyval, w_gate, w_up)

    chunks = cuts(width)
    first = down_part(hidden, w_down, 0, chunks // 2)
    arrived = lax.all_to_all(projected, "gx", split_axis=0, concat_axis=0, tiled=True)
    arrived, first = lax.optimization_barrier((arrived, first))
    arrived = arrived.reshape(devices, steps, rows, -1).transpose(2, 1, 0, 3)
    query = arrived[..., :query_cols].reshape(rows, steps, -1, head)
    keyval = arrived[..., query_cols:].reshape(rows, steps, 2 * head)
    angle_pos = (positions[:, None] + jnp.arange(steps)[None, :]).astype(F32)
    rotated = rotate(query, angle_pos[:, :, None]).astype(BF16)
    new_keys = rotate(keyval[..., :head], angle_pos).astype(BF16)
    new_values = keyval[..., head:].astype(BF16)
    attended = attend(rotated, new_keys, new_values, cache_keys, cache_values, lengths)
    attended = attended.reshape(rows, steps, devices, -1).transpose(2, 1, 0, 3)
    attended = attended.reshape(devices, batch, -1)
    attended, hidden = lax.optimization_barrier((attended, hidden))
    attended = lax.all_to_all(attended, "gx", split_axis=0, concat_axis=0, tiled=True)

    second = down_part(hidden, w_down, chunks // 2, chunks)
    keep, send = branch_parts(attended, first, second, w_out)
    branch = scatter_sums(keep, swap(send, 1, devices), batch, devices)
    result = (own_tokens.astype(F32) + branch).astype(BF16)
    return result.reshape(tokens.shape)


def solution(mesh):
    in_specs = (
        P(None, ("groups", "gx"), None),
        P(),
        P("gx", None),
        P("gx", None),
        P("gx", None),
        P("gx", None),
        P("gx", None),
        P("gx", None),
        P(("groups", "gx"), None, None),
        P(("groups", "gx"), None, None),
        P(("groups", "gx")),
        P(("groups", "gx")),
    )
    out_specs = P(None, ("groups", "gx"), None)
    return jax.shard_map(local, mesh=mesh, in_specs=in_specs, out_specs=out_specs, check_vma=False)
```

```python
import functools
import math

import jax
import jax.numpy as jnp
from jax import lax
from jax.experimental import pallas as pl
from jax.experimental.pallas import tpu as pltpu
from jax.sharding import PartitionSpec as P

F32 = jnp.float32
BF16 = jnp.bfloat16
NT = (((1,), (1,)), ((), ()))
ANY = pl.BlockSpec(memory_space=pl.ANY)
VMEM = pl.BlockSpec(memory_space=pltpu.VMEM)


def params(mib):
    return pltpu.CompilerParams(vmem_limit_bytes=mib << 20)


def cost(rows, *weights):
    size = sum(math.prod(w.shape) for w in weights)
    return pl.CostEstimate(flops=2 * rows * size, bytes_accessed=2 * size, transcendentals=0)


def slot_at(place, half):
    return 2 * place if place < half else 2 * (place - half) + 1


def cuts(width):
    for count in (8, 9, 6, 4, 3, 2):
        if width % (128 * count) == 0:
            return count
    return 1


def center_kernel(tokens_ref, out_ref):
    values = tokens_ref[...].astype(F32)
    centered = values - jnp.mean(values, axis=-1, keepdims=True)
    spread = jnp.mean(centered * centered, axis=-1, keepdims=True)
    out_ref[...] = centered / jnp.sqrt(spread + 1e-05)


def gain_kernel(values_ref, gain_ref, out_ref):
    out_ref[...] = (values_ref[...] * gain_ref[...]).astype(BF16)


def layer_norm(tokens, norm_gain):
    centered = pl.pallas_call(
        center_kernel,
        out_shape=jax.ShapeDtypeStruct(tokens.shape, F32),
        compiler_params=params(4),
        cost_estimate=pl.CostEstimate(
            flops=25 * 10**9, bytes_accessed=75 * 10**6, transcendentals=0
        ),
    )(tokens)
    return pl.pallas_call(
        gain_kernel,
        out_shape=jax.ShapeDtypeStruct(tokens.shape, BF16),
        compiler_params=params(4),
    )(centered, norm_gain.reshape(1, -1))


def project_kernel(
    chunks, even_ref, odd_ref, wq_ref, wg_ref, wu_ref, wk_ref, out_ref, hidden_ref,
    rows, acc, query, gate, sem_u, sem_k, *streams,
):
    half, steps, width = even_ref.shape
    step = width // chunks
    units = wu_ref.shape[0]
    q_cols = wq_ref.shape[0]

    def cols(c):
        return pl.ds(c * step, step)

    slots = streams[0].shape[0]

    def keyval_place(c):
        if len(streams) == 2:
            return streams[1].at[c % slots]
        return streams[0].at[c % slots, pl.ds(units, wk_ref.shape[0])]

    def up_place(c):
        if len(streams) == 2:
            return streams[0].at[c % slots]
        return streams[0].at[c % slots, pl.ds(0, units)]

    copies = [
        (
            pltpu.make_async_copy(wu_ref.at[:, cols(c)], up_place(c), sem_u.at[c]),
            pltpu.make_async_copy(wk_ref.at[:, cols(c)], keyval_place(c), sem_k.at[c]),
        )
        for c in range(chunks)
    ]
    for pair in copies[:slots]:
        for copy in pair:
            copy.start()
    acc[...] = jnp.zeros_like(acc)
    for c in range(chunks):
        part = slice(c * step, (c + 1) * step)
        for p in range(half):
            rows[p * steps : (p + 1) * steps, part] = even_ref[p, :, part]
            q = half + p
            rows[q * steps : (q + 1) * steps, part] = odd_ref[p, :, part]
        block = rows[:, part]
        for total, weight in ((query, wq_ref), (gate, wg_ref)):
            product = lax.dot_general(block, weight[:, part], NT, preferred_element_type=F32)
            total[...] = product if c == 0 else total[...] + product
    for c in range(chunks):
        for copy in copies[c]:
            copy.wait()
        first = 0
        for stream in streams:
            last = first + stream.shape[1]
            acc[:, first:last] += lax.dot_general(
                rows[:, c * step : (c + 1) * step], stream[c % slots], NT, preferred_element_type=F32
            )
            first = last
        if c + slots < chunks:
            for copy in copies[c + slots]:
                copy.start()
    me = lax.axis_index("gx")
    for p in range(2 * half):
        owner = lax.bitwise_xor(me, slot_at(p, half))
        out_ref[owner, :, :q_cols] = query[p * steps : (p + 1) * steps, :]
        out_ref[owner, :, q_cols:] = acc[p * steps : (p + 1) * steps, units:]
    hidden_ref[...] = (jax.nn.silu(gate[...]) * acc[:, :units]).astype(BF16)


def project(even, odd, w_query, w_keyval, w_gate, w_up):
    half, steps, width = even.shape
    n = 2 * half * steps
    chunks = cuts(width)
    step = width // chunks
    q_cols, k_cols, units = w_query.shape[0], w_keyval.shape[0], w_up.shape[0]
    together = k_cols % 16 == 0 and units % 16 == 0
    sizes = [units + k_cols] if together else [units, k_cols]
    slots = min(chunks, 4)
    taken = 2 * slots * step * (units + k_cols) + 6 * n * width + 4 * n * (step + 4 * units)
    near = 2 * width * (q_cols + units)
    taken += near if near < 8 << 20 else 0
    return pl.pallas_call(
        functools.partial(project_kernel, chunks),
        in_specs=[VMEM, VMEM, VMEM, VMEM, ANY, ANY],
        out_specs=[VMEM, VMEM],
        out_shape=[
            jax.ShapeDtypeStruct((2 * half, steps, q_cols + k_cols), F32),
            jax.ShapeDtypeStruct((n, units), BF16),
        ],
        scratch_shapes=[
            pltpu.VMEM((n, width), BF16),
            pltpu.VMEM((n, units + k_cols), F32),
            pltpu.VMEM((n, q_cols), F32),
            pltpu.VMEM((n, units), F32),
            pltpu.SemaphoreType.DMA((chunks,)),
            pltpu.SemaphoreType.DMA((chunks,)),
        ]
        + [pltpu.VMEM((slots, size, step), BF16) for size in sizes],
        compiler_params=params((taken >> 20) + 3),
        cost_estimate=cost(n, w_query, w_keyval, w_gate, w_up),
    )(even, odd, w_query, w_gate, w_up, w_keyval)


def down_kernel(chunks, offset, hidden_ref, w_ref, out_ref, w, out, w_sem, out_sem):
    step = out_ref.shape[1] // chunks

    def cols(c):
        return pl.ds(c * step, step)

    copies = [
        pltpu.make_async_copy(
            w_ref.at[:, pl.ds(offset + c * step, step)], w.at[c], w_sem.at[c]
        )
        for c in range(chunks)
    ]
    out_copies = [
        pltpu.make_async_copy(out.at[c], out_ref.at[:, cols(c)], out_sem.at[c])
        for c in range(chunks)
    ]
    for copy in copies:
        copy.start()
    for c in range(chunks):
        copies[c].wait()
        out[c] = jnp.dot(hidden_ref[...], w[c], preferred_element_type=F32)
        out_copies[c].start()
    for copy in out_copies:
        copy.wait()


def down_part(hidden, w_down, first, last):
    n, units = hidden.shape
    step = w_down.shape[1] // cuts(w_down.shape[1])
    chunks = last - first
    width = chunks * step
    return pl.pallas_call(
        functools.partial(down_kernel, chunks, first * step),
        in_specs=[VMEM, ANY],
        out_specs=ANY,
        out_shape=jax.ShapeDtypeStruct((n, width), F32),
        scratch_shapes=[
            pltpu.VMEM((chunks, units, step), BF16),
            pltpu.VMEM((chunks, n, step), F32),
            pltpu.SemaphoreType.DMA((chunks,)),
            pltpu.SemaphoreType.DMA((chunks,)),
        ],
        compiler_params=params(40),
        cost_estimate=pl.CostEstimate(
            flops=2 * n * units * width, bytes_accessed=2 * units * width, transcendentals=0
        ),
    )(hidden, w_down)


def branch_kernel(
    chunks, attended_ref, first_ref, second_ref, w_ref, keep_ref, send_ref,
    spread, w, part, keep, send, w_sem, part_sem, keep_sem, send_sem,
):
    slots, steps, _ = attended_ref.shape
    half = keep_ref.shape[0]
    step = w_ref.shape[1] // chunks
    middle = first_ref.shape[1] // step
    me = lax.axis_index("gx")

    def cols(c):
        return pl.ds(c * step, step)

    def part_at(c):
        return first_ref.at[:, cols(c)] if c < middle else second_ref.at[:, cols(c - middle)]

    copies = [
        (
            pltpu.make_async_copy(w_ref.at[:, cols(c)], w.at[c], w_sem.at[c]),
            pltpu.make_async_copy(part_at(c), part.at[c], part_sem.at[c]),
        )
        for c in range(chunks)
    ]
    out_copies = [
        (
            pltpu.make_async_copy(keep.at[c], keep_ref.at[:, cols(c)], keep_sem.at[c]),
            pltpu.make_async_copy(send.at[c], send_ref.at[:, cols(c)], send_sem.at[c]),
        )
        for c in range(chunks)
    ]
    for w_copy, part_copy in copies:
        w_copy.start()
        part_copy.start()
    for p in range(slots):
        owner = lax.bitwise_xor(me, slot_at(p, slots // 2))
        spread[p * steps : (p + 1) * steps, :] = attended_ref[owner].astype(F32)
    attended = spread[...].astype(BF16)
    for c in range(chunks):
        for copy in copies[c]:
            copy.wait()
        total = part[c] + jnp.dot(attended, w[c], preferred_element_type=F32)
        keep[c] = total[:half]
        send[c] = total[half:].astype(BF16)
        for copy in out_copies[c]:
            copy.start()
    for pair in out_copies:
        for copy in pair:
            copy.wait()


def branch_parts(attended, first, second, w_out):
    slots, steps, features = attended.shape
    n, width = first.shape[0], w_out.shape[1]
    half = n // 2
    chunks = cuts(width)
    step = width // chunks
    return pl.pallas_call(
        functools.partial(branch_kernel, chunks),
        in_specs=[VMEM, ANY, ANY, ANY],
        out_specs=[ANY, ANY],
        out_shape=[
            jax.ShapeDtypeStruct((half, width), F32),
            jax.ShapeDtypeStruct((half, width), BF16),
        ],
        scratch_shapes=[
            pltpu.VMEM((n, features), F32),
            pltpu.VMEM((chunks, features, step), BF16),
            pltpu.VMEM((chunks, n, step), F32),
            pltpu.VMEM((chunks, half, step), F32),
            pltpu.VMEM((chunks, half, step), BF16),
            pltpu.SemaphoreType.DMA((chunks,)),
            pltpu.SemaphoreType.DMA((chunks,)),
            pltpu.SemaphoreType.DMA((chunks,)),
            pltpu.SemaphoreType.DMA((chunks,)),
        ],
        compiler_params=params(40),
        cost_estimate=cost(n, w_out),
    )(attended, first, second, w_out)


def cut_kernel(plan, keep_ref, came_ref, own_ref, far_ref, *send_refs):
    near, kept, sent = plan
    steps = own_ref.shape[0]
    total = keep_ref[...] + came_ref[...].astype(F32)

    def piece(place):
        return total[place * steps : (place + 1) * steps]

    own_ref[...] = piece(0)
    for k, place in enumerate(kept):
        far_ref[k] = piece(place)
    for place, send_ref in zip(near, send_refs):
        send_ref[...] = piece(place).astype(BF16)
    for group, send_ref in zip(sent, send_refs[len(near) :]):
        for k, place in enumerate(group):
            send_ref[k] = piece(place).astype(BF16)


def cut_parts(keep, came, steps, plan):
    half, width = keep.shape
    near, kept, sent = plan
    chunks = 3 if width % 384 == 0 else 1
    step = width // chunks
    whole = pl.BlockSpec((half, step), lambda c: (0, c))
    piece = pl.BlockSpec((steps, step), lambda c: (0, c))
    pair = pl.BlockSpec((len(kept), steps, step), lambda c: (0, 0, c))
    pair_shape = (len(kept), steps, width)
    return pl.pallas_call(
        functools.partial(cut_kernel, plan),
        grid=(chunks,),
        in_specs=[whole, whole],
        out_specs=[piece, pair] + [piece] * len(near) + [pair] * len(sent),
        out_shape=[
            jax.ShapeDtypeStruct((steps, width), F32),
            jax.ShapeDtypeStruct(pair_shape, F32),
        ]
        + [jax.ShapeDtypeStruct((steps, width), BF16)] * len(near)
        + [jax.ShapeDtypeStruct(pair_shape, BF16)] * len(sent),
        compiler_params=params(32),
        cost_estimate=pl.CostEstimate(
            flops=2 * half * width, bytes_accessed=8 * half * width, transcendentals=0
        ),
    )(keep, came)


def far_kernel(far_ref, *refs):
    count = far_ref.shape[0]
    for k in range(count):
        total = far_ref[k]
        for came_ref in refs[:-count]:
            total = total + came_ref[k].astype(F32)
        refs[len(refs) - count + k][...] = total.astype(BF16)


def far_parts(far, arrived):
    count, steps, width = far.shape
    chunks = 3 if width % 384 == 0 else 1
    step = width // chunks
    pair = pl.BlockSpec((count, steps, step), lambda c: (0, 0, c))
    piece = pl.BlockSpec((steps, step), lambda c: (0, c))
    return pl.pallas_call(
        far_kernel,
        grid=(chunks,),
        in_specs=[pair] * (1 + len(arrived)),
        out_specs=[piece] * count,
        out_shape=[jax.ShapeDtypeStruct((steps, width), BF16)] * count,
        compiler_params=params(32),
        cost_estimate=pl.CostEstimate(
            flops=far.size, bytes_accessed=8 * far.size, transcendentals=0
        ),
    )(far, *arrived)


def rotate(vector, angle_pos):
    half = vector.shape[-1] // 2
    freq = jnp.exp(-math.log(10000.0) * jnp.arange(half, dtype=F32) / half)
    angle = angle_pos[..., None] * freq
    first = vector[..., :half]
    second = vector[..., half:]
    return jnp.concatenate(
        [
            first * jnp.cos(angle) - second * jnp.sin(angle),
            second * jnp.cos(angle) + first * jnp.sin(angle),
        ],
        axis=-1,
    )


def attend(queries, new_keys, new_values, cache_keys, cache_values, lengths):
    steps = queries.shape[1]
    scale = 1.0 / math.sqrt(queries.shape[-1])
    cached = jnp.einsum("rthd,rld->rthl", queries, cache_keys, preferred_element_type=F32) * scale
    live = jnp.arange(cache_keys.shape[1])[None, None, None, :] < lengths[:, None, None, None]
    cached = jnp.where(live, cached, -1e30)
    fresh = jnp.einsum("rthd,red->rthe", queries, new_keys, preferred_element_type=F32) * scale
    known = jnp.arange(steps)[None, :] <= jnp.arange(steps)[:, None]
    fresh = jnp.where(known[None, :, None, :], fresh, -1e30)
    top = jnp.maximum(jnp.max(cached, axis=-1), jnp.max(fresh, axis=-1))
    cached_exp = jnp.exp(cached - top[..., None])
    fresh_exp = jnp.exp(fresh - top[..., None])
    total = jnp.sum(cached_exp, axis=-1) + jnp.sum(fresh_exp, axis=-1)
    cached_w = (cached_exp / total[..., None]).astype(BF16)
    fresh_w = (fresh_exp / total[..., None]).astype(BF16)
    result = jnp.einsum("rthl,rld->rthd", cached_w, cache_values, preferred_element_type=F32)
    result = result + jnp.einsum("rthe,red->rthd", fresh_w, new_values, preferred_element_type=F32)
    return result.astype(BF16)


def swap(value, bits, devices):
    return lax.ppermute(value, "gx", [(i, i ^ bits) for i in range(devices)])


def gather_rows(piece, devices):
    outer = min(4, devices // 2)
    inner = devices // (2 * outer)
    near = [piece] + [swap(piece, 2 * inner * a, devices) for a in range(1, outer)]
    far = [near] + [[swap(p, 2 * b, devices) for p in near] for b in range(1, inner)]
    even = jnp.stack([far[b][a] for a in range(outer) for b in range(inner)])
    return even, swap(even, 1, devices)


def scatter_sums(keep, came, batch, devices):
    outer = min(4, devices // 2)
    inner = devices // (2 * outer)
    middle = outer // 2
    near = [p for p in range(1, middle * inner)]
    kept = [a * inner for a in range(middle, outer)]
    sent = [[p + b for p in kept] for b in range(1, inner)]
    own, far, *sends = cut_parts(keep, came, batch, (near, kept, sent))
    arrived = [
        swap(group, 2 * b, devices) for b, group in zip(range(1, inner), sends[len(near) :])
    ]
    parts = [swap(piece, 2 * p, devices) for p, piece in zip(near, sends)]
    late = [swap(piece, 2 * p, devices) for p, piece in zip(kept, far_parts(far, arrived))]
    for part in parts + late:
        own = own + part.astype(F32)
    return own


def local(
    tokens,
    norm_gain,
    w_query,
    w_keyval,
    w_gate,
    w_up,
    w_out,
    w_down,
    cache_keys,
    cache_values,
    lengths,
    positions,
):
    steps, rows, width = tokens.shape
    head = cache_keys.shape[2]
    query_cols = w_query.shape[0]
    devices = lax.axis_size("gx")
    batch = steps * rows
    own_tokens = tokens.reshape(batch, width)
    even, odd = gather_rows(layer_norm(own_tokens, norm_gain), devices)
    projected, hidden = project(even, odd, w_query, w_keyval, w_gate, w_up)

    chunks = cuts(width)
    first = down_part(hidden, w_down, 0, chunks // 2)
    arrived = lax.all_to_all(projected, "gx", split_axis=0, concat_axis=0, tiled=True)
    arrived, first = lax.optimization_barrier((arrived, first))
    arrived = arrived.reshape(devices, steps, rows, -1).transpose(2, 1, 0, 3)
    query = arrived[..., :query_cols].reshape(rows, steps, -1, head)
    keyval = arrived[..., query_cols:].reshape(rows, steps, 2 * head)
    angle_pos = (positions[:, None] + jnp.arange(steps)[None, :]).astype(F32)
    rotated = rotate(query, angle_pos[:, :, None]).astype(BF16)
    new_keys = rotate(keyval[..., :head], angle_pos).astype(BF16)
    new_values = keyval[..., head:].astype(BF16)
    attended = attend(rotated, new_keys, new_values, cache_keys, cache_values, lengths)
    attended = attended.reshape(rows, steps, devices, -1).transpose(2, 1, 0, 3)
    attended = attended.reshape(devices, batch, -1)
    attended, hidden = lax.optimization_barrier((attended, hidden))
    attended = lax.all_to_all(attended, "gx", split_axis=0, concat_axis=0, tiled=True)

    second = down_part(hidden, w_down, chunks // 2, chunks)
    keep, send = branch_parts(attended, first, second, w_out)
    branch = scatter_sums(keep, swap(send, 1, devices), batch, devices)
    result = (own_tokens.astype(F32) + branch).astype(BF16)
    return result.reshape(tokens.shape)


def solution(mesh):
    in_specs = (
        P(None, ("groups", "gx"), None),
        P(),
        P("gx", None),
        P("gx", None),
        P("gx", None),
        P("gx", None),
        P("gx", None),
        P("gx", None),
        P(("groups", "gx"), None, None),
        P(("groups", "gx"), None, None),
        P(("groups", "gx")),
        P(("groups", "gx")),
    )
    out_specs = P(None, ("groups", "gx"), None)
    return jax.shard_map(local, mesh=mesh, in_specs=in_specs, out_specs=out_specs, check_vma=False)
```

```python
import functools
import math

import jax
import jax.numpy as jnp
from jax import lax
from jax.experimental import pallas as pl
from jax.experimental.pallas import tpu as pltpu
from jax.sharding import PartitionSpec as P

F32 = jnp.float32
BF16 = jnp.bfloat16
NT = (((1,), (1,)), ((), ()))
ANY = pl.BlockSpec(memory_space=pl.ANY)
VMEM = pl.BlockSpec(memory_space=pltpu.VMEM)


def params(mib):
    return pltpu.CompilerParams(vmem_limit_bytes=mib << 20)


def cost(rows, *weights):
    size = sum(math.prod(w.shape) for w in weights)
    return pl.CostEstimate(flops=2 * rows * size, bytes_accessed=2 * size, transcendentals=0)


def slot_at(place, half):
    return 2 * place if place < half else 2 * (place - half) + 1


def cuts(width):
    for count in (8, 9, 6, 4, 3, 2):
        if width % (128 * count) == 0:
            return count
    return 1


def center_kernel(tokens_ref, out_ref):
    values = tokens_ref[...].astype(F32)
    centered = values - jnp.mean(values, axis=-1, keepdims=True)
    spread = jnp.mean(centered * centered, axis=-1, keepdims=True)
    out_ref[...] = centered / jnp.sqrt(spread + 1e-05)


def gain_kernel(values_ref, gain_ref, out_ref):
    out_ref[...] = (values_ref[...] * gain_ref[...]).astype(BF16)


def layer_norm(tokens, norm_gain):
    centered = pl.pallas_call(
        center_kernel,
        out_shape=jax.ShapeDtypeStruct(tokens.shape, F32),
        compiler_params=params(4),
        cost_estimate=pl.CostEstimate(
            flops=25 * 10**9, bytes_accessed=75 * 10**6, transcendentals=0
        ),
    )(tokens)
    return pl.pallas_call(
        gain_kernel,
        out_shape=jax.ShapeDtypeStruct(tokens.shape, BF16),
        compiler_params=params(4),
    )(centered, norm_gain.reshape(1, -1))


def project_kernel(
    chunks, even_ref, odd_ref, wq_ref, wg_ref, wu_ref, wk_ref, out_ref, hidden_ref,
    rows, acc, query, gate, sem_u, sem_k, *streams,
):
    half, steps, width = even_ref.shape
    step = width // chunks
    units = wu_ref.shape[0]
    q_cols = wq_ref.shape[0]

    def cols(c):
        return pl.ds(c * step, step)

    slots = streams[0].shape[0]

    def keyval_place(c):
        if len(streams) == 2:
            return streams[1].at[c % slots]
        return streams[0].at[c % slots, pl.ds(units, wk_ref.shape[0])]

    def up_place(c):
        if len(streams) == 2:
            return streams[0].at[c % slots]
        return streams[0].at[c % slots, pl.ds(0, units)]

    copies = [
        (
            pltpu.make_async_copy(wu_ref.at[:, cols(c)], up_place(c), sem_u.at[c]),
            pltpu.make_async_copy(wk_ref.at[:, cols(c)], keyval_place(c), sem_k.at[c]),
        )
        for c in range(chunks)
    ]
    for pair in copies[:slots]:
        for copy in pair:
            copy.start()
    acc[...] = jnp.zeros_like(acc)
    for c in range(chunks):
        part = slice(c * step, (c + 1) * step)
        for p in range(half):
            rows[p * steps : (p + 1) * steps, part] = even_ref[p, :, part]
            q = half + p
            rows[q * steps : (q + 1) * steps, part] = odd_ref[p, :, part]
        block = rows[:, part]
        for total, weight in ((query, wq_ref), (gate, wg_ref)):
            product = lax.dot_general(block, weight[:, part], NT, preferred_element_type=F32)
            total[...] = product if c == 0 else total[...] + product
    for c in range(chunks):
        for copy in copies[c]:
            copy.wait()
        first = 0
        for stream in streams:
            last = first + stream.shape[1]
            acc[:, first:last] += lax.dot_general(
                rows[:, c * step : (c + 1) * step], stream[c % slots], NT, preferred_element_type=F32
            )
            first = last
        if c + slots < chunks:
            for copy in copies[c + slots]:
                copy.start()
    me = lax.axis_index("gx")
    for p in range(2 * half):
        owner = lax.bitwise_xor(me, slot_at(p, half))
        out_ref[owner, :, :q_cols] = query[p * steps : (p + 1) * steps, :]
        out_ref[owner, :, q_cols:] = acc[p * steps : (p + 1) * steps, units:]
    hidden_ref[...] = (jax.nn.silu(gate[...]) * acc[:, :units]).astype(BF16)


def project(even, odd, w_query, w_keyval, w_gate, w_up):
    half, steps, width = even.shape
    n = 2 * half * steps
    chunks = cuts(width)
    step = width // chunks
    q_cols, k_cols, units = w_query.shape[0], w_keyval.shape[0], w_up.shape[0]
    together = k_cols % 16 == 0 and units % 16 == 0
    sizes = [units + k_cols] if together else [units, k_cols]
    slots = min(chunks, 4)
    taken = 2 * slots * step * (units + k_cols) + 6 * n * width + 4 * n * (step + 4 * units)
    near = 2 * width * (q_cols + units)
    taken += near if near < 8 << 20 else 0
    return pl.pallas_call(
        functools.partial(project_kernel, chunks),
        in_specs=[VMEM, VMEM, VMEM, VMEM, ANY, ANY],
        out_specs=[VMEM, VMEM],
        out_shape=[
            jax.ShapeDtypeStruct((2 * half, steps, q_cols + k_cols), F32),
            jax.ShapeDtypeStruct((n, units), BF16),
        ],
        scratch_shapes=[
            pltpu.VMEM((n, width), BF16),
            pltpu.VMEM((n, units + k_cols), F32),
            pltpu.VMEM((n, q_cols), F32),
            pltpu.VMEM((n, units), F32),
            pltpu.SemaphoreType.DMA((chunks,)),
            pltpu.SemaphoreType.DMA((chunks,)),
        ]
        + [pltpu.VMEM((slots, size, step), BF16) for size in sizes],
        compiler_params=params((taken >> 20) + 3),
        cost_estimate=cost(n, w_query, w_keyval, w_gate, w_up),
    )(even, odd, w_query, w_gate, w_up, w_keyval)


def down_kernel(chunks, offset, hidden_ref, w_ref, out_ref, w, out, w_sem, out_sem):
    step = out_ref.shape[1] // chunks

    def cols(c):
        return pl.ds(c * step, step)

    copies = [
        pltpu.make_async_copy(
            w_ref.at[:, pl.ds(offset + c * step, step)], w.at[c], w_sem.at[c]
        )
        for c in range(chunks)
    ]
    out_copies = [
        pltpu.make_async_copy(out.at[c], out_ref.at[:, cols(c)], out_sem.at[c])
        for c in range(chunks)
    ]
    for copy in copies:
        copy.start()
    for c in range(chunks):
        copies[c].wait()
        out[c] = jnp.dot(hidden_ref[...], w[c], preferred_element_type=F32)
        out_copies[c].start()
    for copy in out_copies:
        copy.wait()


def down_part(hidden, w_down, first, last):
    n, units = hidden.shape
    step = w_down.shape[1] // cuts(w_down.shape[1])
    chunks = last - first
    width = chunks * step
    return pl.pallas_call(
        functools.partial(down_kernel, chunks, first * step),
        in_specs=[VMEM, ANY],
        out_specs=ANY,
        out_shape=jax.ShapeDtypeStruct((n, width), F32),
        scratch_shapes=[
            pltpu.VMEM((chunks, units, step), BF16),
            pltpu.VMEM((chunks, n, step), F32),
            pltpu.SemaphoreType.DMA((chunks,)),
            pltpu.SemaphoreType.DMA((chunks,)),
        ],
        compiler_params=params(40),
        cost_estimate=pl.CostEstimate(
            flops=2 * n * units * width, bytes_accessed=2 * units * width, transcendentals=0
        ),
    )(hidden, w_down)


def branch_kernel(
    chunks, attended_ref, first_ref, second_ref, w_ref, keep_ref, send_ref,
    spread, w, part, keep, send, w_sem, part_sem, keep_sem, send_sem,
):
    slots, steps, _ = attended_ref.shape
    half = keep_ref.shape[0]
    step = w_ref.shape[1] // chunks
    middle = first_ref.shape[1] // step
    me = lax.axis_index("gx")

    def cols(c):
        return pl.ds(c * step, step)

    def part_at(c):
        return first_ref.at[:, cols(c)] if c < middle else second_ref.at[:, cols(c - middle)]

    copies = [
        (
            pltpu.make_async_copy(w_ref.at[:, cols(c)], w.at[c], w_sem.at[c]),
            pltpu.make_async_copy(part_at(c), part.at[c], part_sem.at[c]),
        )
        for c in range(chunks)
    ]
    out_copies = [
        (
            pltpu.make_async_copy(keep.at[c], keep_ref.at[:, cols(c)], keep_sem.at[c]),
            pltpu.make_async_copy(send.at[c], send_ref.at[:, cols(c)], send_sem.at[c]),
        )
        for c in range(chunks)
    ]
    for w_copy, part_copy in copies:
        w_copy.start()
        part_copy.start()
    for p in range(slots):
        owner = lax.bitwise_xor(me, slot_at(p, slots // 2))
        spread[p * steps : (p + 1) * steps, :] = attended_ref[owner].astype(F32)
    attended = spread[...].astype(BF16)
    for c in range(chunks):
        for copy in copies[c]:
            copy.wait()
        total = part[c] + jnp.dot(attended, w[c], preferred_element_type=F32)
        keep[c] = total[:half]
        send[c] = total[half:].astype(BF16)
        for copy in out_copies[c]:
            copy.start()
    for pair in out_copies:
        for copy in pair:
            copy.wait()


def branch_parts(attended, first, second, w_out):
    slots, steps, features = attended.shape
    n, width = first.shape[0], w_out.shape[1]
    half = n // 2
    chunks = cuts(width)
    step = width // chunks
    return pl.pallas_call(
        functools.partial(branch_kernel, chunks),
        in_specs=[VMEM, ANY, ANY, ANY],
        out_specs=[ANY, ANY],
        out_shape=[
            jax.ShapeDtypeStruct((half, width), F32),
            jax.ShapeDtypeStruct((half, width), BF16),
        ],
        scratch_shapes=[
            pltpu.VMEM((n, features), F32),
            pltpu.VMEM((chunks, features, step), BF16),
            pltpu.VMEM((chunks, n, step), F32),
            pltpu.VMEM((chunks, half, step), F32),
            pltpu.VMEM((chunks, half, step), BF16),
            pltpu.SemaphoreType.DMA((chunks,)),
            pltpu.SemaphoreType.DMA((chunks,)),
            pltpu.SemaphoreType.DMA((chunks,)),
            pltpu.SemaphoreType.DMA((chunks,)),
        ],
        compiler_params=params(40),
        cost_estimate=cost(n, w_out),
    )(attended, first, second, w_out)


def cut_kernel(plan, keep_ref, came_ref, own_ref, far_ref, *send_refs):
    near, kept, sent = plan
    steps = own_ref.shape[0]
    total = keep_ref[...] + came_ref[...].astype(F32)

    def piece(place):
        return total[place * steps : (place + 1) * steps]

    own_ref[...] = piece(0)
    for k, place in enumerate(kept):
        far_ref[k] = piece(place)
    for place, send_ref in zip(near, send_refs):
        send_ref[...] = piece(place).astype(BF16)
    for group, send_ref in zip(sent, send_refs[len(near) :]):
        for k, place in enumerate(group):
            send_ref[k] = piece(place).astype(BF16)


def cut_parts(keep, came, steps, plan):
    half, width = keep.shape
    near, kept, sent = plan
    chunks = 3 if width % 384 == 0 else 1
    step = width // chunks
    whole = pl.BlockSpec((half, step), lambda c: (0, c))
    piece = pl.BlockSpec((steps, step), lambda c: (0, c))
    pair = pl.BlockSpec((len(kept), steps, step), lambda c: (0, 0, c))
    pair_shape = (len(kept), steps, width)
    return pl.pallas_call(
        functools.partial(cut_kernel, plan),
        grid=(chunks,),
        in_specs=[whole, whole],
        out_specs=[piece, pair] + [piece] * len(near) + [pair] * len(sent),
        out_shape=[
            jax.ShapeDtypeStruct((steps, width), F32),
            jax.ShapeDtypeStruct(pair_shape, F32),
        ]
        + [jax.ShapeDtypeStruct((steps, width), BF16)] * len(near)
        + [jax.ShapeDtypeStruct(pair_shape, BF16)] * len(sent),
        compiler_params=params(32),
        cost_estimate=pl.CostEstimate(
            flops=2 * half * width, bytes_accessed=8 * half * width, transcendentals=0
        ),
    )(keep, came)


def far_kernel(far_ref, *refs):
    count = far_ref.shape[0]
    for k in range(count):
        total = far_ref[k]
        for came_ref in refs[:-count]:
            total = total + came_ref[k].astype(F32)
        refs[len(refs) - count + k][...] = total.astype(BF16)


def far_parts(far, arrived):
    count, steps, width = far.shape
    chunks = 3 if width % 384 == 0 else 1
    step = width // chunks
    pair = pl.BlockSpec((count, steps, step), lambda c: (0, 0, c))
    piece = pl.BlockSpec((steps, step), lambda c: (0, c))
    return pl.pallas_call(
        far_kernel,
        grid=(chunks,),
        in_specs=[pair] * (1 + len(arrived)),
        out_specs=[piece] * count,
        out_shape=[jax.ShapeDtypeStruct((steps, width), BF16)] * count,
        compiler_params=params(32),
        cost_estimate=pl.CostEstimate(
            flops=far.size, bytes_accessed=8 * far.size, transcendentals=0
        ),
    )(far, *arrived)


def rotate(vector, angle_pos):
    half = vector.shape[-1] // 2
    freq = jnp.exp(-math.log(10000.0) * jnp.arange(half, dtype=F32) / half)
    angle = angle_pos[..., None] * freq
    first = vector[..., :half]
    second = vector[..., half:]
    return jnp.concatenate(
        [
            first * jnp.cos(angle) - second * jnp.sin(angle),
            second * jnp.cos(angle) + first * jnp.sin(angle),
        ],
        axis=-1,
    )


def attend(queries, new_keys, new_values, cache_keys, cache_values, lengths):
    steps = queries.shape[1]
    scale = 1.0 / math.sqrt(queries.shape[-1])
    cached = jnp.einsum("rthd,rld->rthl", queries, cache_keys, preferred_element_type=F32) * scale
    live = jnp.arange(cache_keys.shape[1])[None, None, None, :] < lengths[:, None, None, None]
    cached = jnp.where(live, cached, -1e30)
    fresh = jnp.einsum("rthd,red->rthe", queries, new_keys, preferred_element_type=F32) * scale
    known = jnp.arange(steps)[None, :] <= jnp.arange(steps)[:, None]
    fresh = jnp.where(known[None, :, None, :], fresh, -1e30)
    top = jnp.maximum(jnp.max(cached, axis=-1), jnp.max(fresh, axis=-1))
    cached_exp = jnp.exp(cached - top[..., None])
    fresh_exp = jnp.exp(fresh - top[..., None])
    total = jnp.sum(cached_exp, axis=-1) + jnp.sum(fresh_exp, axis=-1)
    cached_w = (cached_exp / total[..., None]).astype(BF16)
    fresh_w = (fresh_exp / total[..., None]).astype(BF16)
    result = jnp.einsum("rthl,rld->rthd", cached_w, cache_values, preferred_element_type=F32)
    result = result + jnp.einsum("rthe,red->rthd", fresh_w, new_values, preferred_element_type=F32)
    return result.astype(BF16)


def swap(value, bits, devices):
    return lax.ppermute(value, "gx", [(i, i ^ bits) for i in range(devices)])


def gather_rows(piece, devices):
    outer = min(4, devices // 2)
    inner = devices // (2 * outer)
    middle = outer // 2
    stride = 2 * inner
    far = [swap(piece, stride * a, devices) for a in reversed(range(middle, outer))][::-1]
    pieces = {(a, 0): far[a - middle] for a in range(middle, outer)}
    for b in range(inner):
        for a in range(middle):
            pieces[a, b] = swap(piece, stride * a + 2 * b, devices) if a or b else piece
    for b in range(1, inner):
        passed = swap(jnp.stack(far), 2 * b, devices)
        pieces.update({(a, b): passed[a - middle] for a in range(middle, outer)})
    even = jnp.stack([pieces[a, b] for a in range(outer) for b in range(inner)])
    return even, swap(even, 1, devices)


def scatter_sums(keep, came, batch, devices):
    outer = min(4, devices // 2)
    inner = devices // (2 * outer)
    middle = outer // 2
    near = [p for p in range(1, middle * inner)]
    kept = [a * inner for a in range(middle, outer)]
    sent = [[p + b for p in kept] for b in range(1, inner)]
    own, far, *sends = cut_parts(keep, came, batch, (near, kept, sent))
    arrived = [
        swap(group, 2 * b, devices) for b, group in zip(range(1, inner), sends[len(near) :])
    ]
    parts = [swap(piece, 2 * p, devices) for p, piece in zip(near, sends)]
    late = [swap(piece, 2 * p, devices) for p, piece in zip(kept, far_parts(far, arrived))]
    for part in parts + late:
        own = own + part.astype(F32)
    return own


def local(
    tokens,
    norm_gain,
    w_query,
    w_keyval,
    w_gate,
    w_up,
    w_out,
    w_down,
    cache_keys,
    cache_values,
    lengths,
    positions,
):
    steps, rows, width = tokens.shape
    head = cache_keys.shape[2]
    query_cols = w_query.shape[0]
    devices = lax.axis_size("gx")
    batch = steps * rows
    own_tokens = tokens.reshape(batch, width)
    even, odd = gather_rows(layer_norm(own_tokens, norm_gain), devices)
    projected, hidden = project(even, odd, w_query, w_keyval, w_gate, w_up)

    chunks = cuts(width)
    first = down_part(hidden, w_down, 0, chunks // 2)
    arrived = lax.all_to_all(projected, "gx", split_axis=0, concat_axis=0, tiled=True)
    arrived, first = lax.optimization_barrier((arrived, first))
    arrived = arrived.reshape(devices, steps, rows, -1).transpose(2, 1, 0, 3)
    query = arrived[..., :query_cols].reshape(rows, steps, -1, head)
    keyval = arrived[..., query_cols:].reshape(rows, steps, 2 * head)
    angle_pos = (positions[:, None] + jnp.arange(steps)[None, :]).astype(F32)
    rotated = rotate(query, angle_pos[:, :, None]).astype(BF16)
    new_keys = rotate(keyval[..., :head], angle_pos).astype(BF16)
    new_values = keyval[..., head:].astype(BF16)
    attended = attend(rotated, new_keys, new_values, cache_keys, cache_values, lengths)
    attended = attended.reshape(rows, steps, devices, -1).transpose(2, 1, 0, 3)
    attended = attended.reshape(devices, batch, -1)
    attended, hidden = lax.optimization_barrier((attended, hidden))
    attended = lax.all_to_all(attended, "gx", split_axis=0, concat_axis=0, tiled=True)

    second = down_part(hidden, w_down, chunks // 2, chunks)
    keep, send = branch_parts(attended, first, second, w_out)
    branch = scatter_sums(keep, swap(send, 1, devices), batch, devices)
    result = (own_tokens.astype(F32) + branch).astype(BF16)
    return result.reshape(tokens.shape)


def solution(mesh):
    in_specs = (
        P(None, ("groups", "gx"), None),
        P(),
        P("gx", None),
        P("gx", None),
        P("gx", None),
        P("gx", None),
        P("gx", None),
        P("gx", None),
        P(("groups", "gx"), None, None),
        P(("groups", "gx"), None, None),
        P(("groups", "gx")),
        P(("groups", "gx")),
    )
    out_specs = P(None, ("groups", "gx"), None)
    return jax.shard_map(local, mesh=mesh, in_specs=in_specs, out_specs=out_specs, check_vma=False)
```
